128 devices in a mesh: sar: 8 (over y, core), opt: 16 (over z, x).
Axes of the slice: x: 4, y: 4, z: 4, core: 2. Of those that a mesh axis runs over, the one named last changes fastest.
Arguments:
- sar_tokens: bfloat16 [2048, 196, 512], P(('sar', 'opt')), may hold values from -600 to 600
- opt_tokens: bfloat16 [2048, 196, 512], P(('sar', 'opt')), may hold values from -600 to 600
- candidates: int32 [2048, 3], P(('sar', 'opt')), may hold values from 0 to 2047, as said below
Outputs:
- grad_sar: bfloat16 [2048, 196, 512], P(('sar', 'opt'))
- grad_opt: bfloat16 [2048, 196, 512], P(('sar', 'opt'))
The draws below stay inside these ranges and needn't reach their ends.
Inputs may be any that keep to these rules, and one draw needn't show every extreme that they name: `candidates`: row i lists optical tiles of the same block of 256 tiles as SAR tile i (ids b * 256 to b * 256 + 255), never a tile of the aligned group of 16 tiles that holds i. Over one aligned group of 16 SAR tiles the lists name at most 2 distinct tiles of any other group, and exactly 2 of some group; ids may repeat.
All inputs are finite; a program needn't handle non-finite values.
Results may differ from the reference program's by a relative error of at most 0.0061.
Values may be sent and summed in bfloat16 or wider, within the bound.
A program may use at most 192 MiB of HBM per device.

```python
import math
import jax
import jax.numpy as jnp
from jax import lax

D = 512
L = 196
TILE_DEV = 16
NEG = 3
CAP = 2
BLOCK = 256
TILES = 2048
N_SAR = 8
N_OPT = 16


def shared_field(key):
    normal_key = jax.random.fold_in(key, 0)
    gain_key = jax.random.fold_in(key, 2)
    shape = (TILES, L, D)
    normal_part = jax.random.truncated_normal(normal_key, -4.0, 4.0, shape, jnp.float32)
    gains = jnp.exp(jax.random.uniform(gain_key, shape, jnp.float32) * math.log(10.0))
    return normal_part * gains


def draw_sar_tokens(key, part):
    common = shared_field(key)
    top_scale = 10.0
    key = jax.random.fold_in(key, 1)
    row_scale = jnp.exp(jax.random.uniform(key, (TILES, L, 1), jnp.float32) * math.log(top_scale))
    return (row_scale * common).astype(jnp.bfloat16)


def draw_opt_tokens(key, part):
    common = shared_field(key)
    top_scale = 10.0
    key = jax.random.fold_in(key, 2)
    noise_key = jax.random.fold_in(key, 0)
    gain_key = jax.random.fold_in(key, 2)
    row_key = jax.random.fold_in(key, 3)
    shape = (TILES, L, D)
    noise = jax.random.truncated_normal(noise_key, -4.0, 4.0, shape, jnp.float32)
    gains = jnp.exp(jax.random.uniform(gain_key, shape, jnp.float32) * math.log(10.0))
    row_scale = jnp.exp(jax.random.uniform(row_key, (TILES, L, 1), jnp.float32) * math.log(top_scale))
    return (row_scale * (0.31 * common + noise * gains)).astype(jnp.bfloat16)


def draw_candidates(key, part):
    key = jax.random.fold_in(key, 3)
    devices = N_SAR * N_OPT
    block_size = TILE_DEV * N_OPT
    requests = TILE_DEV * NEG
    pool_length = (N_OPT - 1) * CAP

    def per_device(device):
        device_key = jax.random.fold_in(key, device)
        count_key, owner_key, first_key, pick_key, order_key = jax.random.split(device_key, 5)
        own_group = device % N_OPT
        block_index = device // N_OPT
        others = (own_group + jnp.arange(1, N_OPT)) % N_OPT
        counts = jax.random.randint(count_key, (N_OPT - 1,), 0, CAP + 1)
        hot_owner = jax.random.randint(owner_key, (), 0, N_OPT - 1)
        counts = jnp.where(jnp.arange(N_OPT - 1) == hot_owner, CAP, counts)
        first_tile = jax.random.randint(first_key, (N_OPT - 1,), 0, TILE_DEV)
        tile_ids = (first_tile[:, None] + jnp.arange(CAP)[None, :]) % TILE_DEV
        pool_ids = (block_index * block_size + others[:, None] * TILE_DEV + tile_ids).reshape(-1)
        usable = (jnp.arange(CAP)[None, :] < counts[:, None]).reshape(-1).astype(jnp.int32)
        pool_size = jnp.sum(usable)
        pick_rank = jax.random.randint(pick_key, (requests,), 0, pool_size)
        valid_rank = jnp.cumsum(usable) - 1
        matches = (usable[None, :] == 1) & (valid_rank[None, :] == pick_rank[:, None])
        chosen = jnp.sum(jnp.where(matches, pool_ids[None, :], 0), axis=1)
        forced = jnp.arange(requests) < CAP
        forced_pos = jnp.clip(hot_owner * CAP + jnp.arange(requests), 0, pool_length - 1)
        chosen = jnp.where(forced, pool_ids[forced_pos], chosen)
        shuffle = jax.random.permutation(order_key, requests)
        return chosen[shuffle].reshape(TILE_DEV, NEG)
    table = jax.vmap(per_device)(jnp.arange(devices))
    return table.reshape(devices * TILE_DEV, NEG).astype(jnp.int32)


def setup_inputs(seed: int = 0) -> dict:
    key_list = jax.random.split(jax.random.key(seed), 4)
    sar_tokens = draw_sar_tokens(jax.random.fold_in(key_list[3], 71), 0)
    opt_tokens = draw_opt_tokens(jax.random.fold_in(key_list[3], 71), 0)
    candidates = draw_candidates(jax.random.fold_in(key_list[3], 71), 0)
    return dict(sar_tokens=sar_tokens, opt_tokens=opt_tokens, candidates=candidates)


EPSILON = 1e-06
POOL_TEMP = 0.02
CAND_TEMP = 0.1
NCE_TEMP = 0.07
LOSS_SCALE = 256.0
NCE_SCALE = 0.05 * 256.0 / 0.07

def unit_rows(tokens):
    values = tokens.astype(jnp.float32)
    inverse = lax.rsqrt(lax.optimization_barrier(jnp.sum(values * values, axis=-1, keepdims=True)) + EPSILON)
    return (values * inverse, inverse)

def pooled_unit(unit_tokens):
    mean_rows = lax.optimization_barrier(jnp.mean(unit_tokens, axis=1))
    pool_scale = lax.rsqrt(lax.optimization_barrier(jnp.sum(mean_rows * mean_rows, axis=-1, keepdims=True)) + EPSILON)
    return (mean_rows * pool_scale, pool_scale)

def pair_grads(sar_rows, cand_rows):
    sar_wide = sar_rows.astype(jnp.float32)
    cand_wide = cand_rows.astype(jnp.float32)
    scores = jnp.einsum('ad,kbd->kab', sar_wide, cand_wide)
    exponent = jnp.exp(scores / POOL_TEMP)
    totals = lax.optimization_barrier(jnp.sum(exponent, axis=-1))
    match_score = POOL_TEMP * lax.optimization_barrier(jnp.mean(jnp.log(totals), axis=-1))
    cand_weight = jnp.exp(match_score / CAND_TEMP)
    cand_prob = cand_weight / jnp.sum(cand_weight)
    target = (jnp.arange(cand_prob.shape[0]) == 0).astype(jnp.float32)
    pair_coef = LOSS_SCALE * (cand_prob - target) / CAND_TEMP
    length = sar_rows.shape[0]
    weights = ((pair_coef / length)[:, None, None] * exponent / totals[:, :, None]).astype(jnp.bfloat16)
    weights_wide = weights.astype(jnp.float32)
    sar_part = jnp.einsum('kab,kbd->ad', weights_wide, cand_wide)
    cand_part = jnp.einsum('kab,ad->kbd', weights_wide, sar_wide)
    return (sar_part, cand_part)

def finish(unit_tokens, inverse, pool_rows, pool_scale, pair_grad, pool_grad):
    length = unit_tokens.shape[1]
    pooled_back = (pool_grad - pool_rows * lax.optimization_barrier(jnp.sum(pool_rows * pool_grad, axis=-1, keepdims=True))) * pool_scale
    total = pair_grad + pooled_back[:, None, :] / length
    back = (total - unit_tokens * lax.optimization_barrier(jnp.sum(unit_tokens * total, axis=-1, keepdims=True))) * inverse
    return back.astype(jnp.bfloat16)

def reference(sar_tokens, opt_tokens, candidates):
    sar_blocks = sar_tokens.reshape(N_SAR, BLOCK, L, D)
    opt_blocks = opt_tokens.reshape(N_SAR, BLOCK, L, D)
    cand_blocks = candidates.reshape(N_SAR, BLOCK, NEG)

    def pool_block(tokens):
        unit_tokens, unused = unit_rows(tokens)
        return pooled_unit(unit_tokens)
    sar_pool, sar_scale = lax.map(pool_block, sar_blocks)
    opt_pool, opt_scale = lax.map(pool_block, opt_blocks)
    sar_pool = sar_pool.reshape(TILES, D)
    opt_pool = opt_pool.reshape(TILES, D)
    sar_round = sar_pool.astype(jnp.bfloat16)
    opt_round = opt_pool.astype(jnp.bfloat16)
    logits = jnp.dot(sar_round, opt_round.T, preferred_element_type=jnp.float32) / NCE_TEMP
    exp_logits = jnp.exp(logits)
    nce_prob = exp_logits / lax.optimization_barrier(jnp.sum(exp_logits, axis=1, keepdims=True))
    identity = jnp.eye(TILES, dtype=jnp.float32)
    nce_coef = (NCE_SCALE * (nce_prob - identity)).astype(jnp.bfloat16)
    sar_pool_grad = jnp.dot(nce_coef, opt_round, preferred_element_type=jnp.float32)
    opt_pool_grad = jnp.dot(nce_coef.T, sar_round, preferred_element_type=jnp.float32)

    def block_grads(inputs):
        sar_block, opt_block, cand_block, sar_pg, opt_pg, sar_pp, opt_pp, sar_ps, opt_ps = inputs
        sar_unit, sar_inverse = unit_rows(sar_block)
        opt_unit, opt_inverse = unit_rows(opt_block)
        sar_bf = sar_unit.astype(jnp.bfloat16)
        opt_bf = opt_unit.astype(jnp.bfloat16)
        local_ids = (cand_block % BLOCK).astype(jnp.int32)
        cand_lists = jnp.concatenate([jnp.arange(BLOCK).astype(jnp.int32)[:, None], local_ids], axis=1)
        row_group = (jnp.arange(BLOCK) // TILE_DEV).astype(jnp.int32)

        def pair_step(opt_sums, inputs_row):
            sar_rows, cand_row = inputs_row
            sar_part, cand_part = pair_grads(sar_rows, opt_bf[cand_row])
            return (opt_sums.at[cand_row].add(cand_part), sar_part)

        def group_step(running, inputs_group):
            group_id, sar_group, cand_group = inputs_group
            start_sums = jnp.zeros((BLOCK, L, D), jnp.float32)
            group_sums, sar_part = lax.scan(pair_step, start_sums, (sar_group, cand_group))
            rounded = lax.optimization_barrier(group_sums.astype(jnp.bfloat16)).astype(jnp.float32)
            own_rows = (row_group == group_id)[:, None, None]
            return (running + jnp.where(own_rows, group_sums, rounded), sar_part)
        start_total = jnp.zeros((BLOCK, L, D), jnp.float32)
        opt_pair, sar_pair = lax.scan(group_step, start_total, (jnp.arange(N_OPT).astype(jnp.int32), sar_bf.reshape(N_OPT, TILE_DEV, L, D), cand_lists.reshape(N_OPT, TILE_DEV, NEG + 1)))
        sar_pair = sar_pair.reshape(BLOCK, L, D)
        grad_sar_block = finish(sar_unit, sar_inverse, sar_pp, sar_ps, sar_pair, sar_pg)
        grad_opt_block = finish(opt_unit, opt_inverse, opt_pp, opt_ps, opt_pair, opt_pg)
        return (grad_sar_block, grad_opt_block)
    grad_sar, grad_opt = lax.map(block_grads, (sar_blocks, opt_blocks, cand_blocks, sar_pool_grad.reshape(N_SAR, BLOCK, D), opt_pool_grad.reshape(N_SAR, BLOCK, D), sar_pool.reshape(N_SAR, BLOCK, D), opt_pool.reshape(N_SAR, BLOCK, D), sar_scale.reshape(N_SAR, BLOCK, 1), opt_scale.reshape(N_SAR, BLOCK, 1)))
    return (grad_sar.reshape(TILES, L, D), grad_opt.reshape(TILES, L, D))
```

```python
import functools

import jax
import jax.numpy as jnp
from jax import lax
from jax.experimental import pallas as pl
from jax.experimental.pallas import tpu as pltpu
from jax.sharding import PartitionSpec as P

NEG = 3
CAP = 2
EPSILON = 1e-06
POOL_TEMP = 0.02
CAND_TEMP = 0.1
NCE_TEMP = 0.07
LOSS_SCALE = 256.0
NCE_SCALE = 0.05 * 256.0 / 0.07
LOG2E = 1.4426950408889634

T = 16
L = 196
D = 512
MAIN = 192
ROWS = 208
LANES = 256
PAIRS = T * NEG
GROUPS = 16
SIDE = 4
SLOTS = (GROUPS - 1) * CAP
CHUNK = 48
CHUNKS = MAIN // CHUNK
HALF = D // 2
FIRST = 3 * CHUNK
ORDER = [10, 2, 8, 6, 14, 9, 11, 5, 7, 13, 15, 1, 3, 4, 12]

SLOT_AT, PAIR_AT, TILE_AT, SAME_AT, LAST_AT, TABLE = 0, 48, 96, 144, 192, 256

BF16 = jnp.bfloat16
F32 = jnp.float32


def negated(turn):
    return ((SIDE - turn // SIDE) % SIDE) * SIDE + (SIDE - turn % SIDE) % SIDE


def dot(a, b, dims):
    return lax.dot_general(a, b, (dims, ((), ())), preferred_element_type=F32)


NN, NT, TN = ((1,), (0,)), ((1,), (1,)), ((0,), (0,))


def inverse_norm(rows):
    return lax.rsqrt(jnp.sum(rows * rows, axis=-1, keepdims=True) + EPSILON)


def finish_rows(raw, back, pair):
    inverse = inverse_norm(raw)
    unit = raw * inverse
    total = pair + back
    return ((total - unit * jnp.sum(unit * total, axis=-1, keepdims=True)) * inverse).astype(BF16)


def kernel(
    n_sar, table, ids, sar_raw, opt_raw, sar_out, opt_out,
    sar_rows, opt_rows, outbox, out_tail, fetched, fetched_end, fetched_tail, weight, parts, acc,
    returned, returned_tail, tail_sums, pools, sums, own_pair, means, pool_rows, backs, totals,
    scale, tail_buf, ids_in, ids_smem, keys, ranks, order2, same2, last2,
    ids_send, ids_recv, ids_sem, fetch_send, fetch_recv, back_send, back_recv,
    plane_send, plane_recv, block_send, block_recv, write_sem,
):
    my_sar = lax.axis_index("sar")
    me = lax.axis_index("opt")
    my_z, my_x = me // SIDE, me % SIDE

    def peer(turn):
        z = (my_z + turn // SIDE) % SIDE
        x = (my_x + turn % SIDE) % SIDE
        return {"opt": z * SIDE + x}

    def sar_peer(step):
        return {"sar": (my_sar + step) % n_sar}

    def remote(src, dst, send, recv, to):
        return pltpu.make_async_remote_copy(
            src_ref=src, dst_ref=dst, send_sem=send, recv_sem=recv,
            device_id=to, device_id_type=pl.DeviceIdType.MESH,
        )

    barrier = pltpu.get_barrier_semaphore()
    for turn in range(1, GROUPS):
        pl.semaphore_signal(
            barrier, inc=1, device_id=peer(turn), device_id_type=pl.DeviceIdType.MESH
        )
    for step in range(1, n_sar):
        pl.semaphore_signal(
            barrier, inc=1, device_id=sar_peer(step), device_id_type=pl.DeviceIdType.MESH
        )

    tail_buf[...] = jnp.zeros_like(tail_buf)

    def normalize(which, raw, rows):
        def tile(i, carry):
            main = raw[i, 0:MAIN].astype(F32)
            tail_buf[0:4] = raw[i, MAIN:L].astype(F32)
            tail = tail_buf[...]
            unit = main * inverse_norm(main)
            unit_tail = tail * inverse_norm(tail)
            rows[i, 0:MAIN] = unit.astype(BF16)
            rows[i, MAIN:ROWS] = unit_tail.astype(BF16)
            mean = (
                jnp.sum(unit, axis=0, keepdims=True) + jnp.sum(unit_tail, axis=0, keepdims=True)
            ) * (1.0 / L)
            means[which, pl.ds(i, 1), :] = mean
            return carry

        lax.fori_loop(0, T, tile, 0)

    normalize(1, opt_raw, opt_rows)

    pl.semaphore_wait(barrier, GROUPS - 1 + n_sar - 1)

    def ids_copy(turn):
        return remote(
            ids.at[turn], ids_in.at[turn], ids_send.at[turn], ids_recv.at[turn], peer(turn)
        )

    for turn in ORDER:
        ids_copy(turn).start()
    for turn in ORDER:
        ids_copy(turn).wait()
    to_smem = pltpu.make_async_copy(ids_in, ids_smem, ids_sem)
    to_smem.start()
    to_smem.wait()

    def fetch_copy(turn, c):
        box = pl.ds((turn - 1) * CAP, CAP)
        if c == CHUNKS:
            src, dst = out_tail.at[turn - 1], fetched_tail.at[turn - 1]
        else:
            at = pl.ds(c * CHUNK, CHUNK)
            src = outbox.at[box, at]
            if c * CHUNK < FIRST:
                dst = fetched.at[box, at]
            else:
                dst = fetched_end.at[box, pl.ds(c * CHUNK - FIRST, CHUNK)]
        return remote(src, dst, fetch_send.at[turn, c], fetch_recv.at[turn, c], peer(turn))

    for c in range(CHUNKS + 1):
        for turn in ORDER:
            asker = negated(turn)
            if c < CHUNKS:
                for s in range(CAP):
                    outbox[(turn - 1) * CAP + s, c * CHUNK : (c + 1) * CHUNK] = opt_rows[
                        ids_smem[asker, 0, s], c * CHUNK : (c + 1) * CHUNK
                    ]
            else:
                ends = [
                    opt_rows[ids_smem[asker, 0, s], MAIN:ROWS].astype(F32)[0:8] for s in range(CAP)
                ]
                out_tail[turn - 1] = jnp.concatenate(ends, axis=0).astype(BF16)
            fetch_copy(turn, c).start()

    def clear(i, carry):
        sar_rows[i, ROWS:LANES] = jnp.zeros((LANES - ROWS, D), BF16)
        return carry

    lax.fori_loop(0, T, clear, 0)
    normalize(0, sar_raw, sar_rows)

    mine = pl.ds(pl.multiple_of(me * T, T), T)
    for which in range(2):
        mean = means[which]
        pool_scale = lax.rsqrt(jnp.sum(mean * mean, axis=-1, keepdims=True) + EPSILON)
        pool = mean * pool_scale
        pool_rows[which] = pool
        pools[my_sar, which, mine, :] = pool.astype(BF16)

    def plane_copy(turn):
        here = pools.at[my_sar, :, mine, :]
        return remote(here, here, plane_send.at[turn], plane_recv.at[turn], peer(turn))

    for turn in ORDER:
        plane_copy(turn).start()

    def exp_scores(rows, i):
        return jnp.exp2(dot(rows, sar_rows[i], NT) * (LOG2E / POOL_TEMP))

    live = lax.broadcasted_iota(jnp.int32, (ROWS, LANES), 0) < L

    def own_scores(i, carry):
        e = exp_scores(opt_rows[i], i)
        weight[i] = e.astype(BF16)
        totals[0, pl.ds(i, 1), :] = jnp.sum(jnp.where(live, e, 0.0), axis=0, keepdims=True)
        return carry

    lax.fori_loop(0, T, own_scores, 0)

    for p in range(SLOTS):
        keys[p] = ids_smem[p // CAP + 1, 0, p % CAP] * 32 + p

    def rank_of(p, carry):
        key = keys[p]
        rank = jnp.int32(0)
        for q in range(SLOTS):
            rank += (keys[q] < key).astype(jnp.int32)
        ranks[p] = rank
        return carry

    lax.fori_loop(0, SLOTS, rank_of, 0)

    def place_of(t, before):
        key = jnp.int32(0)
        for p in range(SLOTS):
            key += jnp.where(ranks[p] == t, keys[p], 0)
        tile = key // 32
        order2[t] = key % 32
        same2[t] = (tile == before).astype(jnp.int32)
        return tile

    lax.fori_loop(0, SLOTS, place_of, jnp.int32(-1))

    def last_of(j, before):
        upto = jnp.int32(0)
        for p in range(SLOTS):
            upto += (keys[p] < (j + 1) * 32).astype(jnp.int32)
        last2[j] = jnp.where(upto > before, upto - 1, SLOTS)
        return upto

    lax.fori_loop(0, T, last_of, jnp.int32(0))

    for turn in ORDER:
        plane_copy(turn).wait_recv()

    def block_copy(step):
        here = pools.at[my_sar]
        return remote(here, here, block_send.at[step], block_recv.at[step], sar_peer(step))

    for step in range(1, n_sar):
        block_copy(step).start()

    for c in range(FIRST // CHUNK):
        for turn in ORDER:
            fetch_copy(turn, c).wait_recv()

    def first_scores(i, carry):
        for k in range(NEG):
            e = exp_scores(fetched[table[SLOT_AT + i * NEG + k]], i)
            weight[T + i * NEG + k, 0:FIRST] = e.astype(BF16)
            totals[k + 1, pl.ds(i, 1), :] = jnp.sum(e, axis=0, keepdims=True)
        return carry

    lax.fori_loop(0, T, first_scores, 0)

    for c in range(FIRST // CHUNK, CHUNKS + 1):
        for turn in ORDER:
            fetch_copy(turn, c).wait_recv()
    for turn in range(1, GROUPS):
        ends = fetched_tail[turn - 1].astype(F32)
        for s in range(CAP):
            end = ends[8 * s : 8 * s + 8]
            fetched_end[(turn - 1) * CAP + s, MAIN - FIRST :] = jnp.concatenate(
                [end, jnp.zeros_like(end)], axis=0
            ).astype(BF16)

    live_end = lax.broadcasted_iota(jnp.int32, (ROWS - FIRST, LANES), 0) < L - FIRST

    def last_scores(i, carry):
        for k in range(NEG):
            e = exp_scores(fetched_end[table[SLOT_AT + i * NEG + k]], i)
            weight[T + i * NEG + k, FIRST:ROWS] = e.astype(BF16)
            totals[k + 1, pl.ds(i, 1), :] += jnp.sum(
                jnp.where(live_end, e, 0.0), axis=0, keepdims=True
            )
        return carry

    lax.fori_loop(0, T, last_scores, 0)

    tokens = lax.broadcasted_iota(jnp.int32, (T, LANES), 1) < L
    cand = []
    for k in range(NEG + 1):
        logs = jnp.where(tokens, jnp.log(totals[k]), 0.0)
        match = (POOL_TEMP / L) * jnp.sum(logs, axis=-1, keepdims=True)
        cand.append(jnp.exp(match / CAND_TEMP))
    cand_sum = cand[0] + cand[1] + cand[2] + cand[3]
    for k in range(NEG + 1):
        coef = LOSS_SCALE * (cand[k] / cand_sum - (1.0 if k == 0 else 0.0)) / CAND_TEMP
        scaled = (coef / L) / totals[k]
        for i in range(T):
            scale[i if k == 0 else T + i * NEG + k - 1] = scaled[i : i + 1]

    def weights(p):
        return (weight[p].astype(F32) * scale[p]).astype(BF16)

    def back_copy(turn, h, c):
        box = pl.ds((turn - 1) * CAP, CAP)
        if c is None:
            src, dst = out_tail.at[turn - 1], returned_tail.at[turn - 1]
            sem = 2 * CHUNKS
        else:
            at, cols = pl.ds(c * CHUNK, CHUNK), pl.ds(h * HALF, HALF)
            src, dst = outbox.at[box, at, cols], returned[c].at[box, :, cols]
            sem = h * CHUNKS + c
        return remote(src, dst, back_send.at[turn, sem], back_recv.at[turn, sem], peer(turn))

    parts[PAIRS] = jnp.zeros((ROWS, HALF), BF16)
    for c in range(CHUNKS + 1):
        for turn in ORDER:
            fetch_copy(turn, c).wait_send()
    for h in range(2):
        cols = slice(h * HALF, (h + 1) * HALF)
        acc[...] = jnp.zeros_like(acc)

        def add_pair(p, carry, cols=cols):
            pair = table[PAIR_AT + p]
            keep = table[SAME_AT + p].astype(F32)
            part = dot(weights(T + pair), sar_rows[table[TILE_AT + p], :, cols], NN)
            total = acc[...] * keep + part
            acc[...] = total
            parts[p] = total.astype(BF16)
            return carry

        lax.fori_loop(0, PAIRS, add_pair, 0)

        for c in range(CHUNKS):
            at = slice(c * CHUNK, (c + 1) * CHUNK)
            for turn in ORDER:
                for s in range(CAP):
                    last = table[LAST_AT + (negated(turn) - 1) * CAP + s]
                    outbox[(turn - 1) * CAP + s, at, cols] = parts[last, at, :]
                back_copy(turn, h, c).start()
        for turn in ORDER:
            ends = [
                parts[table[LAST_AT + (negated(turn) - 1) * CAP + s], MAIN:ROWS].astype(F32)[0:8]
                for s in range(CAP)
            ]
            out_tail[turn - 1, :, cols] = jnp.concatenate(ends, axis=0).astype(BF16)
            if h:
                back_copy(turn, h, None).start()

    for step in range(1, n_sar):
        block_copy(step).wait_recv()
    block = pools.shape[2]
    logit_scale = LOG2E / NCE_TEMP
    own_sar = pools[my_sar, 0, mine, :]
    own_opt = pools[my_sar, 1, mine, :]

    def own_rows(t, row_sums):
        e = jnp.exp2(dot(own_sar, pools[t, 1], NT) * logit_scale)
        return row_sums + jnp.sum(e, axis=-1, keepdims=True)

    row_sums = lax.fori_loop(0, n_sar, own_rows, jnp.zeros((T, 1), F32))

    def own_coefs(t, grad):
        e = jnp.exp2(dot(own_sar, pools[t, 1], NT) * logit_scale)
        rows = my_sar * block + me * T + lax.broadcasted_iota(jnp.int32, (T, block), 0)
        columns = t * block + lax.broadcasted_iota(jnp.int32, (T, block), 1)
        diagonal = (rows == columns).astype(F32)
        coefs = (NCE_SCALE * (e / row_sums - diagonal)).astype(BF16)
        return grad + dot(coefs, pools[t, 1], NN)

    sar_pool_grad = lax.fori_loop(0, n_sar, own_coefs, jnp.zeros((T, D), F32))

    def opt_coefs(s, grad):
        rows_here = pools[s, 0]

        def add_sums(t, sums_here):
            e = jnp.exp2(dot(rows_here, pools[t, 1], NT) * logit_scale)
            return sums_here + jnp.sum(e, axis=-1, keepdims=True)

        sums_here = lax.fori_loop(0, n_sar, add_sums, jnp.zeros((block, 1), F32))
        e = jnp.exp2(dot(rows_here, own_opt, NT) * logit_scale)
        rows = s * block + lax.broadcasted_iota(jnp.int32, (block, T), 0)
        columns = my_sar * block + me * T + lax.broadcasted_iota(jnp.int32, (block, T), 1)
        diagonal = (rows == columns).astype(F32)
        coefs = (NCE_SCALE * (e / sums_here - diagonal)).astype(BF16)
        return grad + dot(coefs, rows_here, TN)

    opt_pool_grad = lax.fori_loop(0, n_sar, opt_coefs, jnp.zeros((T, D), F32))

    for which, grad in enumerate((sar_pool_grad, opt_pool_grad)):
        mean = means[which]
        pool_scale = lax.rsqrt(jnp.sum(mean * mean, axis=-1, keepdims=True) + EPSILON)
        pool = pool_rows[which]
        along = jnp.sum(pool * grad, axis=-1, keepdims=True)
        backs[which] = (grad - pool * along) * pool_scale * (1.0 / L)

    def raw_tail(raw, i):
        tail_buf[0:4] = raw[i, MAIN:L].astype(F32)
        return tail_buf[...]

    def sar_tile(i, carry):
        own = weights(i)
        own_pair[i] = dot(own, sar_rows[i], NN)
        cands = [opt_rows[i]]
        coefs = [own]
        for k in range(NEG):
            cands.append(fetched[table[SLOT_AT + i * NEG + k]])
            cands.append(fetched_end[table[SLOT_AT + i * NEG + k]])
            coefs.append(weights(T + i * NEG + k))
        pair = dot(jnp.concatenate(coefs, axis=0), jnp.concatenate(cands, axis=0), TN)
        back = backs[0, pl.ds(i, 1), :]
        opt_rows[i, 0:MAIN] = finish_rows(sar_raw[i, 0:MAIN].astype(F32), back, pair[0:MAIN])
        opt_rows[i, MAIN:ROWS] = finish_rows(raw_tail(sar_raw, i), back, pair[MAIN:ROWS])
        return carry

    lax.fori_loop(0, T, sar_tile, 0)
    write_sar = pltpu.make_async_copy(opt_rows, sar_out, write_sem.at[CHUNKS + 1])
    write_sar.start()

    sums[SLOTS] = jnp.zeros((CHUNK, D), F32)
    tail_sums[SLOTS] = jnp.zeros((8, D), F32)
    writes = []
    for c in range(CHUNKS):
        at = slice(c * CHUNK, (c + 1) * CHUNK)
        for turn in ORDER:
            back_copy(turn, 0, c).wait_recv()
            back_copy(turn, 1, c).wait_recv()

        def add_slot(t, total, c=c):
            total = total * same2[t].astype(F32) + returned[c][order2[t]].astype(F32)
            sums[t] = total
            return total

        lax.fori_loop(0, SLOTS, add_slot, jnp.zeros((CHUNK, D), F32))

        if c * CHUNK < FIRST:
            stage, stage_at = fetched, c * CHUNK
        else:
            stage, stage_at = fetched_end, c * CHUNK - FIRST

        def opt_tile(j, carry, at=at, stage=stage, stage_at=stage_at):
            pair = own_pair[j, at] + sums[last2[j]]
            stage[j, stage_at : stage_at + CHUNK] = finish_rows(
                opt_raw[j, at].astype(F32), backs[1, pl.ds(j, 1), :], pair
            )
            return carry

        lax.fori_loop(0, T, opt_tile, 0)
        rows_at = pl.ds(c * CHUNK, CHUNK)
        write = pltpu.make_async_copy(
            stage.at[pl.ds(0, T), pl.ds(stage_at, CHUNK)], opt_out.at[:, rows_at], write_sem.at[c]
        )
        write.start()
        writes.append(write)

    for turn in ORDER:
        back_copy(turn, 1, None).wait_recv()

    def add_tail(t, total):
        place = order2[t]
        both = returned_tail[place // CAP].astype(F32)
        second = (place % CAP).astype(F32)
        total = total * same2[t].astype(F32) + both[0:8] * (1.0 - second) + both[8:16] * second
        tail_sums[t] = total
        return total

    lax.fori_loop(0, SLOTS, add_tail, jnp.zeros((8, D), F32))

    def opt_tail(j, carry):
        part = tail_sums[last2[j]]
        pair = own_pair[j, MAIN:ROWS] + jnp.concatenate([part, jnp.zeros_like(part)], axis=0)
        fetched_end[j, MAIN - FIRST :] = finish_rows(raw_tail(opt_raw, j), backs[1, pl.ds(j, 1), :], pair)
        return carry

    lax.fori_loop(0, T, opt_tail, 0)
    rows_at = pl.ds(MAIN, ROWS - MAIN)
    write = pltpu.make_async_copy(
        fetched_end.at[pl.ds(0, T), pl.ds(MAIN - FIRST, ROWS - MAIN)],
        opt_out.at[:, rows_at],
        write_sem.at[CHUNKS],
    )
    write.start()
    writes.append(write)

    for turn in ORDER:
        plane_copy(turn).wait_send()
        for c in range(CHUNKS):
            back_copy(turn, 0, c).wait_send()
            back_copy(turn, 1, c).wait_send()
        back_copy(turn, 1, None).wait_send()
    for step in range(1, n_sar):
        block_copy(step).wait_send()
    write_sar.wait()
    for write in writes:
        write.wait()


def index_tables(candidates):
    me = lax.axis_index("opt")
    block = T * GROUPS
    local_ids = (candidates % block).reshape(-1)
    hits = (local_ids[:, None] == jnp.arange(block)[None, :]).astype(jnp.int32)
    needed = jnp.max(hits, axis=0).reshape(GROUPS, T)
    rank = jnp.cumsum(needed, axis=1) - needed
    chosen = needed[:, :, None] * (rank[:, :, None] == jnp.arange(CAP)[None, None, :])
    asked = jnp.sum(chosen * jnp.arange(T)[None, :, None], axis=1)
    pair_rank = jnp.sum(hits * rank.reshape(-1)[None, :], axis=1)
    owner = local_ids // T
    turn = ((me // SIDE - owner // SIDE) % SIDE) * SIDE + (me % SIDE - owner % SIDE) % SIDE
    slot = (turn - 1) * CAP + pair_rank
    turns = jnp.arange(GROUPS)
    owners = ((me // SIDE + turns // SIDE) % SIDE) * SIDE + (me % SIDE + turns % SIDE) % SIDE
    by_turn = jnp.sum(
        (owners[:, None] == jnp.arange(GROUPS)[None, :])[:, :, None] * asked[None], axis=1
    )
    ids = jnp.zeros((GROUPS, 1, 128), jnp.int32).at[:, 0, :CAP].set(by_turn)
    pairs = jnp.arange(PAIRS)
    key = slot * 64 + pairs
    place = jnp.sum(key[None, :] < key[:, None], axis=1)
    at_place = place[None, :] == pairs[:, None]
    sorted_key = jnp.sum(at_place * key[None, :], axis=1)
    sorted_pair, sorted_slot = sorted_key % 64, sorted_key // 64
    same = (sorted_slot == jnp.concatenate([jnp.full((1,), -1), sorted_slot[:-1]])).astype(jnp.int32)
    slots = jnp.arange(SLOTS)
    upto = jnp.sum(slot[None, :] <= slots[:, None], axis=1)
    used = jnp.any(slot[None, :] == slots[:, None], axis=1)
    last = jnp.where(used, upto - 1, PAIRS)
    table = jnp.concatenate(
        [slot, sorted_pair, sorted_pair // NEG, same, last, jnp.zeros((TABLE - LAST_AT - SLOTS,))]
    )
    return table.astype(jnp.int32), ids


def per_device(n_sar, sar_tokens, opt_tokens, candidates):
    table, ids = index_tables(candidates)
    vmem = pl.BlockSpec(memory_space=pltpu.VMEM)
    dma = pltpu.SemaphoreType.DMA
    padded = jax.ShapeDtypeStruct((T, ROWS, D), BF16)
    grads = pl.pallas_call(
        functools.partial(kernel, n_sar),
        out_shape=(padded, padded),
        in_specs=[pl.BlockSpec(memory_space=pltpu.SMEM), vmem, vmem, vmem],
        out_specs=[pl.BlockSpec(memory_space=pl.ANY)] * 2,
        scratch_shapes=[
            pltpu.VMEM((T, LANES, D), BF16),
            pltpu.VMEM((T, ROWS, D), BF16),
            pltpu.VMEM((SLOTS, MAIN, D), BF16),
            pltpu.VMEM((GROUPS - 1, 16, D), BF16),
            pltpu.VMEM((SLOTS, FIRST, D), BF16),
            pltpu.VMEM((SLOTS, ROWS - FIRST, D), BF16),
            pltpu.VMEM((GROUPS - 1, 16, D), BF16),
            pltpu.VMEM((T + PAIRS, ROWS, LANES), BF16),
            pltpu.VMEM((PAIRS + 1, ROWS, HALF), BF16),
            pltpu.VMEM((ROWS, HALF), F32),
            [pltpu.VMEM((SLOTS, CHUNK, D), BF16)] * CHUNKS,
            pltpu.VMEM((GROUPS - 1, 16, D), BF16),
            pltpu.VMEM((SLOTS + 1, 8, D), F32),
            pltpu.VMEM((n_sar, 2, T * GROUPS, D), BF16),
            pltpu.VMEM((SLOTS + 1, CHUNK, D), F32),
            pltpu.VMEM((T, ROWS, D), F32),
            pltpu.VMEM((2, T, D), F32),
            pltpu.VMEM((2, T, D), F32),
            pltpu.VMEM((2, T, D), F32),
            pltpu.VMEM((NEG + 1, T, LANES), F32),
            pltpu.VMEM((T + PAIRS, 1, LANES), F32),
            pltpu.VMEM((16, D), F32),
            pltpu.VMEM((GROUPS, 1, 128), jnp.int32),
            pltpu.SMEM((GROUPS, 1, 128), jnp.int32),
            pltpu.SMEM((32,), jnp.int32),
            pltpu.SMEM((32,), jnp.int32),
            pltpu.SMEM((32,), jnp.int32),
            pltpu.SMEM((32,), jnp.int32),
            pltpu.SMEM((32,), jnp.int32),
            dma((GROUPS,)),
            dma((GROUPS,)),
            dma,
            dma((GROUPS, CHUNKS + 1)),
            dma((GROUPS, CHUNKS + 1)),
            dma((GROUPS, 2 * CHUNKS + 1)),
            dma((GROUPS, 2 * CHUNKS + 1)),
            dma((GROUPS,)),
            dma((GROUPS,)),
            dma((n_sar,)),
            dma((n_sar,)),
            dma((CHUNKS + 2,)),
        ],
        compiler_params=pltpu.CompilerParams(
            collective_id=0, has_side_effects=True, vmem_limit_bytes=63 * 2**20
        ),
        name="match_grads",
    )(table, ids, sar_tokens, opt_tokens)
    return tuple(grad[:, :L] for grad in grads)


def solution(mesh):
    tiles = P(("sar", "opt"), None, None)
    return jax.shard_map(
        functools.partial(per_device, mesh.shape["sar"]),
        mesh=mesh,
        in_specs=(tiles, tiles, P(("sar", "opt"), None)),
        out_specs=(tiles, tiles),
        check_vma=False,
    )
```

```python
import functools

import jax
import jax.numpy as jnp
from jax import lax
from jax.experimental import pallas as pl
from jax.experimental.pallas import tpu as pltpu
from jax.sharding import PartitionSpec as P

NEG = 3
CAP = 2
EPSILON = 1e-06
POOL_TEMP = 0.02
CAND_TEMP = 0.1
NCE_TEMP = 0.07
LOSS_SCALE = 256.0
NCE_SCALE = 0.05 * 256.0 / 0.07
LOG2E = 1.4426950408889634

T = 16
L = 196
D = 512
MAIN = 192
ROWS = 208
LANES = 256
PAIRS = T * NEG
GROUPS = 16
SIDE = 4
SLOTS = (GROUPS - 1) * CAP
CHUNK = 48
CHUNKS = MAIN // CHUNK
HALF = D // 2
FIRST = 3 * CHUNK
ORDER = [10, 2, 8, 6, 14, 9, 11, 5, 7, 13, 15, 1, 3, 4, 12]

SLOT_AT, PAIR_AT, TILE_AT, SAME_AT, LAST_AT, TABLE = 0, 48, 96, 144, 192, 256

BF16 = jnp.bfloat16
F32 = jnp.float32


def negated(turn):
    return ((SIDE - turn // SIDE) % SIDE) * SIDE + (SIDE - turn % SIDE) % SIDE


def dot(a, b, dims):
    return lax.dot_general(a, b, (dims, ((), ())), preferred_element_type=F32)


NN, NT, TN = ((1,), (0,)), ((1,), (1,)), ((0,), (0,))


def inverse_norm(rows):
    return lax.rsqrt(jnp.sum(rows * rows, axis=-1, keepdims=True) + EPSILON)


def finish_rows(raw, back, pair):
    total = pair + back
    inverse = inverse_norm(raw)
    along = jnp.sum(raw * total, axis=-1, keepdims=True)
    return ((total - raw * (inverse * inverse * along)) * inverse).astype(BF16)


def kernel(
    n_sar, table, ids, sar_raw, opt_raw, sar_out, opt_out,
    sar_rows, opt_rows, outbox, out_tail, fetched, fetched_end, fetched_tail, weight, parts, acc,
    returned, returned_tail, tail_sums, pools, sums, own_pair, means, pool_rows, backs, totals,
    scale, tail_buf, ids_in, ids_smem, keys, ranks, order2, same2, last2,
    ids_send, ids_recv, ids_sem, fetch_send, fetch_recv, back_send, back_recv,
    plane_send, plane_recv, block_send, block_recv, write_sem,
):
    my_sar = lax.axis_index("sar")
    me = lax.axis_index("opt")
    my_z, my_x = me // SIDE, me % SIDE

    def peer(turn):
        z = (my_z + turn // SIDE) % SIDE
        x = (my_x + turn % SIDE) % SIDE
        return {"opt": z * SIDE + x}

    n_y = n_sar // 2
    my_y, my_core = my_sar // 2, my_sar % 2

    def y_peer(step):
        return {"sar": ((my_y + step) % n_y) * 2 + my_core}

    mate = {"sar": my_y * 2 + 1 - my_core}

    def remote(src, dst, send, recv, to):
        return pltpu.make_async_remote_copy(
            src_ref=src, dst_ref=dst, send_sem=send, recv_sem=recv,
            device_id=to, device_id_type=pl.DeviceIdType.MESH,
        )

    barrier = pltpu.get_barrier_semaphore()
    for turn in range(1, GROUPS):
        pl.semaphore_signal(
            barrier, inc=1, device_id=peer(turn), device_id_type=pl.DeviceIdType.MESH
        )
    for step in range(1, n_y):
        pl.semaphore_signal(
            barrier, inc=1, device_id=y_peer(step), device_id_type=pl.DeviceIdType.MESH
        )
    pl.semaphore_signal(barrier, inc=1, device_id=mate, device_id_type=pl.DeviceIdType.MESH)

    tail_buf[...] = jnp.zeros_like(tail_buf)

    def normalize(which, raw, rows):
        def tile(i, carry):
            main = raw[i, 0:MAIN].astype(F32)
            tail_buf[0:4] = raw[i, MAIN:L].astype(F32)
            tail = tail_buf[...]
            unit = main * inverse_norm(main)
            unit_tail = tail * inverse_norm(tail)
            rows[i, 0:MAIN] = unit.astype(BF16)
            rows[i, MAIN:ROWS] = unit_tail.astype(BF16)
            mean = (
                jnp.sum(unit, axis=0, keepdims=True) + jnp.sum(unit_tail, axis=0, keepdims=True)
            ) * (1.0 / L)
            means[which, pl.ds(i, 1), :] = mean
            return carry

        lax.fori_loop(0, T, tile, 0, unroll=2)

    normalize(1, opt_raw, opt_rows)

    pl.semaphore_wait(barrier, GROUPS - 1 + n_y)

    def ids_copy(turn):
        return remote(
            ids.at[turn], ids_in.at[turn], ids_send.at[turn], ids_recv.at[turn], peer(turn)
        )

    for turn in ORDER:
        ids_copy(turn).start()
    for turn in ORDER:
        ids_copy(turn).wait()
    to_smem = pltpu.make_async_copy(ids_in, ids_smem, ids_sem)
    to_smem.start()
    to_smem.wait()

    def fetch_copy(turn, c):
        box = pl.ds((turn - 1) * CAP, CAP)
        if c == CHUNKS:
            src, dst = out_tail.at[turn - 1], fetched_tail.at[turn - 1]
        else:
            at = pl.ds(c * CHUNK, CHUNK)
            src = outbox.at[box, at]
            if c * CHUNK < FIRST:
                dst = fetched.at[box, at]
            else:
                dst = fetched_end.at[box, pl.ds(c * CHUNK - FIRST, CHUNK)]
        return remote(src, dst, fetch_send.at[turn, c], fetch_recv.at[turn, c], peer(turn))

    def send_chunk(c):
        for turn in ORDER:
            asker = negated(turn)
            if c < CHUNKS:
                for s in range(CAP):
                    outbox[(turn - 1) * CAP + s, c * CHUNK : (c + 1) * CHUNK] = opt_rows[
                        ids_smem[asker, 0, s], c * CHUNK : (c + 1) * CHUNK
                    ]
            else:
                ends = [
                    opt_rows[ids_smem[asker, 0, s], MAIN:ROWS].astype(F32)[0:8] for s in range(CAP)
                ]
                out_tail[turn - 1] = jnp.concatenate(ends, axis=0).astype(BF16)
            fetch_copy(turn, c).start()

    send_chunk(0)

    def clear(i, carry):
        sar_rows[i, ROWS:LANES] = jnp.zeros((LANES - ROWS, D), BF16)
        return carry

    lax.fori_loop(0, T, clear, 0)
    normalize(0, sar_raw, sar_rows)

    mine = pl.ds(pl.multiple_of(me * T, T), T)
    for which in range(2):
        mean = means[which]
        pool_scale = lax.rsqrt(jnp.sum(mean * mean, axis=-1, keepdims=True) + EPSILON)
        pool = mean * pool_scale
        pool_rows[which] = pool
        pools[my_y, my_core, which, mine, :] = pool.astype(BF16)

    def plane_copy(turn):
        here = pools.at[my_y, my_core, :, mine, :]
        return remote(here, here, plane_send.at[turn], plane_recv.at[turn], peer(turn))

    for turn in ORDER:
        plane_copy(turn).start()

    send_chunk(1)

    def exp_scores(rows, i):
        return jnp.exp2(dot(rows, sar_rows[i], NT) * (LOG2E / POOL_TEMP))

    live = lax.broadcasted_iota(jnp.int32, (ROWS, LANES), 0) < L

    def own_scores(i, carry):
        e = exp_scores(opt_rows[i], i)
        weight[i] = e.astype(BF16)
        totals[0, pl.ds(i, 1), :] = jnp.sum(jnp.where(live, e, 0.0), axis=0, keepdims=True)
        return carry

    lax.fori_loop(0, T, own_scores, 0)

    for p in range(SLOTS):
        keys[p] = ids_smem[p // CAP + 1, 0, p % CAP] * 32 + p

    def rank_of(p, carry):
        key = keys[p]
        rank = jnp.int32(0)
        for q in range(SLOTS):
            rank += (keys[q] < key).astype(jnp.int32)
        ranks[p] = rank
        return carry

    lax.fori_loop(0, SLOTS, rank_of, 0)

    def place_of(t, before):
        key = jnp.int32(0)
        for p in range(SLOTS):
            key += jnp.where(ranks[p] == t, keys[p], 0)
        tile = key // 32
        order2[t] = key % 32
        same2[t] = (tile == before).astype(jnp.int32)
        return tile

    lax.fori_loop(0, SLOTS, place_of, jnp.int32(-1))

    def last_of(j, before):
        upto = jnp.int32(0)
        for p in range(SLOTS):
            upto += (keys[p] < (j + 1) * 32).astype(jnp.int32)
        last2[j] = jnp.where(upto > before, upto - 1, SLOTS)
        return upto

    lax.fori_loop(0, T, last_of, jnp.int32(0))

    for turn in ORDER:
        plane_copy(turn).wait_recv()

    def block_copy(step):
        here = pools.at[my_y, my_core]
        return remote(here, here, block_send.at[step], block_recv.at[step], y_peer(step))

    def mate_copy(y):
        here = pools.at[y, my_core]
        return remote(here, here, block_send.at[n_y + y], block_recv.at[n_y + y], mate)

    for step in range(1, n_y):
        block_copy(step).start()
        if step + 1 < CHUNKS:
            send_chunk(step + 1)
    for c in range(n_y, CHUNKS + 1):
        send_chunk(c)

    for c in range(FIRST // CHUNK):
        for turn in ORDER:
            fetch_copy(turn, c).wait_recv()

    def first_scores(i, carry):
        rows = [fetched[table[SLOT_AT + i * NEG + k]] for k in range(NEG)]
        exps = exp_scores(jnp.concatenate(rows, axis=0), i)
        for k in range(NEG):
            e = exps[k * FIRST : (k + 1) * FIRST]
            weight[T + i * NEG + k, 0:FIRST] = e.astype(BF16)
            totals[k + 1, pl.ds(i, 1), :] = jnp.sum(e, axis=0, keepdims=True)
        return carry

    lax.fori_loop(0, T, first_scores, 0)

    for c in range(FIRST // CHUNK, CHUNKS + 1):
        for turn in ORDER:
            fetch_copy(turn, c).wait_recv()
    for turn in range(1, GROUPS):
        ends = fetched_tail[turn - 1].astype(F32)
        for s in range(CAP):
            end = ends[8 * s : 8 * s + 8]
            fetched_end[(turn - 1) * CAP + s, MAIN - FIRST :] = jnp.concatenate(
                [end, jnp.zeros_like(end)], axis=0
            ).astype(BF16)

    live_end = lax.broadcasted_iota(jnp.int32, (ROWS - FIRST, LANES), 0) < L - FIRST

    def last_scores(i, carry):
        rows = [fetched_end[table[SLOT_AT + i * NEG + k]] for k in range(NEG)]
        exps = exp_scores(jnp.concatenate(rows, axis=0), i)
        for k in range(NEG):
            e = exps[k * (ROWS - FIRST) : (k + 1) * (ROWS - FIRST)]
            weight[T + i * NEG + k, FIRST:ROWS] = e.astype(BF16)
            totals[k + 1, pl.ds(i, 1), :] += jnp.sum(
                jnp.where(live_end, e, 0.0), axis=0, keepdims=True
            )
        return carry

    lax.fori_loop(0, T, last_scores, 0, unroll=2)

    for step in range(1, n_y):
        block_copy(step).wait_recv()
    for y in range(n_y):
        mate_copy(y).start()

    tokens = lax.broadcasted_iota(jnp.int32, (T, LANES), 1) < L
    cand = []
    for k in range(NEG + 1):
        logs = jnp.where(tokens, jnp.log(totals[k]), 0.0)
        match = (POOL_TEMP / L) * jnp.sum(logs, axis=-1, keepdims=True)
        cand.append(jnp.exp(match / CAND_TEMP))
    cand_sum = cand[0] + cand[1] + cand[2] + cand[3]
    for k in range(NEG + 1):
        coef = LOSS_SCALE * (cand[k] / cand_sum - (1.0 if k == 0 else 0.0)) / CAND_TEMP
        scaled = (coef / L) / totals[k]
        for i in range(T):
            scale[i if k == 0 else T + i * NEG + k - 1] = scaled[i : i + 1]

    def weights(p):
        return (weight[p].astype(F32) * scale[p]).astype(BF16)

    def back_copy(turn, h, c):
        box = pl.ds((turn - 1) * CAP, CAP)
        if c is None:
            src, dst = out_tail.at[turn - 1], returned_tail.at[turn - 1]
            sem = 2 * CHUNKS
        else:
            at, cols = pl.ds(c * CHUNK, CHUNK), pl.ds(h * HALF, HALF)
            src, dst = outbox.at[box, at, cols], returned[c].at[box, :, cols]
            sem = h * CHUNKS + c
        return remote(src, dst, back_send.at[turn, sem], back_recv.at[turn, sem], peer(turn))

    parts[PAIRS] = jnp.zeros((ROWS, HALF), BF16)
    for c in range(CHUNKS + 1):
        for turn in ORDER:
            fetch_copy(turn, c).wait_send()
    for h in range(2):
        cols = slice(h * HALF, (h + 1) * HALF)
        acc[...] = jnp.zeros_like(acc)

        def add_pair(p, carry, cols=cols):
            pair = table[PAIR_AT + p]
            keep = table[SAME_AT + p].astype(F32)
            part = dot(weights(T + pair), sar_rows[table[TILE_AT + p], :, cols], NN)
            total = acc[...] * keep + part
            acc[...] = total
            parts[p] = total.astype(BF16)
            return carry

        lax.fori_loop(0, PAIRS, add_pair, 0, unroll=2)

        def send_tails(h=h, cols=cols):
            for turn in ORDER:
                ends = [
                    parts[table[LAST_AT + (negated(turn) - 1) * CAP + s], MAIN:ROWS].astype(F32)[0:8]
                    for s in range(CAP)
                ]
                out_tail[turn - 1, :, cols] = jnp.concatenate(ends, axis=0).astype(BF16)
                if h:
                    back_copy(turn, h, None).start()

        if h:
            send_tails()
        for c in range(CHUNKS):
            at = slice(c * CHUNK, (c + 1) * CHUNK)
            for turn in ORDER:
                for s in range(CAP):
                    last = table[LAST_AT + (negated(turn) - 1) * CAP + s]
                    outbox[(turn - 1) * CAP + s, at, cols] = parts[last, at, :]
                back_copy(turn, h, c).start()
        if not h:
            send_tails()

    for y in range(n_y):
        mate_copy(y).wait_recv()
    block = pools.shape[3]
    logit_scale = LOG2E / NCE_TEMP
    own_sar = pools[my_y, my_core, 0, mine, :]
    own_opt = pools[my_y, my_core, 1, mine, :]

    def own_rows(t, row_sums):
        e = jnp.exp2(dot(own_sar, pools[t // 2, t % 2, 1], NT) * logit_scale)
        return row_sums + jnp.sum(e, axis=-1, keepdims=True)

    row_sums = lax.fori_loop(0, n_sar, own_rows, jnp.zeros((T, 1), F32))

    def own_coefs(t, grad):
        e = jnp.exp2(dot(own_sar, pools[t // 2, t % 2, 1], NT) * logit_scale)
        rows = my_sar * block + me * T + lax.broadcasted_iota(jnp.int32, (T, block), 0)
        columns = t * block + lax.broadcasted_iota(jnp.int32, (T, block), 1)
        diagonal = (rows == columns).astype(F32)
        coefs = (NCE_SCALE * (e / row_sums - diagonal)).astype(BF16)
        return grad + dot(coefs, pools[t // 2, t % 2, 1], NN)

    sar_pool_grad = lax.fori_loop(0, n_sar, own_coefs, jnp.zeros((T, D), F32))

    def opt_coefs(s, grad):
        rows_here = pools[s // 2, s % 2, 0]

        def add_sums(t, sums_here):
            e = jnp.exp2(dot(rows_here, pools[t // 2, t % 2, 1], NT) * logit_scale)
            return sums_here + jnp.sum(e, axis=-1, keepdims=True)

        sums_here = lax.fori_loop(0, n_sar, add_sums, jnp.zeros((block, 1), F32))
        e = jnp.exp2(dot(rows_here, own_opt, NT) * logit_scale)
        rows = s * block + lax.broadcasted_iota(jnp.int32, (block, T), 0)
        columns = my_sar * block + me * T + lax.broadcasted_iota(jnp.int32, (block, T), 1)
        diagonal = (rows == columns).astype(F32)
        coefs = (NCE_SCALE * (e / sums_here - diagonal)).astype(BF16)
        return grad + dot(coefs, rows_here, TN)

    opt_pool_grad = lax.fori_loop(0, n_sar, opt_coefs, jnp.zeros((T, D), F32))

    for which, grad in enumerate((sar_pool_grad, opt_pool_grad)):
        mean = means[which]
        pool_scale = lax.rsqrt(jnp.sum(mean * mean, axis=-1, keepdims=True) + EPSILON)
        pool = pool_rows[which]
        along = jnp.sum(pool * grad, axis=-1, keepdims=True)
        backs[which] = (grad - pool * along) * pool_scale * (1.0 / L)

    def raw_tail(raw, i):
        tail_buf[0:4] = raw[i, MAIN:L].astype(F32)
        return tail_buf[...]

    def sar_tile(i, carry):
        own = weights(i)
        own_pair[i] = dot(own, sar_rows[i], NN)
        cands = [opt_rows[i]]
        coefs = [own]
        for k in range(NEG):
            cands.append(fetched[table[SLOT_AT + i * NEG + k]])
            cands.append(fetched_end[table[SLOT_AT + i * NEG + k]])
            coefs.append(weights(T + i * NEG + k))
        pair = dot(jnp.concatenate(coefs, axis=0), jnp.concatenate(cands, axis=0), TN)
        back = backs[0, pl.ds(i, 1), :]
        opt_rows[i, 0:MAIN] = finish_rows(sar_raw[i, 0:MAIN].astype(F32), back, pair[0:MAIN])
        opt_rows[i, MAIN:ROWS] = finish_rows(raw_tail(sar_raw, i), back, pair[MAIN:ROWS])
        return carry

    lax.fori_loop(0, T, sar_tile, 0)
    write_sar = pltpu.make_async_copy(opt_rows, sar_out, write_sem.at[CHUNKS + 1])
    write_sar.start()

    sums[SLOTS] = jnp.zeros((CHUNK, D), F32)
    tail_sums[SLOTS] = jnp.zeros((8, D), F32)
    writes = []
    for turn in ORDER:
        back_copy(turn, 1, None).wait_recv()

    def add_tail(t, total):
        place = order2[t]
        both = returned_tail[place // CAP].astype(F32)
        second = (place % CAP).astype(F32)
        total = total * same2[t].astype(F32) + both[0:8] * (1.0 - second) + both[8:16] * second
        tail_sums[t] = total
        return total

    lax.fori_loop(0, SLOTS, add_tail, jnp.zeros((8, D), F32))

    def opt_tail(j, carry):
        part = tail_sums[last2[j]]
        pair = own_pair[j, MAIN:ROWS] + jnp.concatenate([part, jnp.zeros_like(part)], axis=0)
        fetched_end[j, MAIN - FIRST :] = finish_rows(raw_tail(opt_raw, j), backs[1, pl.ds(j, 1), :], pair)
        return carry

    lax.fori_loop(0, T, opt_tail, 0)
    rows_at = pl.ds(MAIN, ROWS - MAIN)
    write = pltpu.make_async_copy(
        fetched_end.at[pl.ds(0, T), pl.ds(MAIN - FIRST, ROWS - MAIN)],
        opt_out.at[:, rows_at],
        write_sem.at[CHUNKS],
    )
    write.start()
    writes.append(write)

    for c in range(CHUNKS):
        at = slice(c * CHUNK, (c + 1) * CHUNK)
        for turn in ORDER:
            back_copy(turn, 0, c).wait_recv()
            back_copy(turn, 1, c).wait_recv()

        def add_slot(t, total, c=c):
            total = total * same2[t].astype(F32) + returned[c][order2[t]].astype(F32)
            sums[t] = total
            return total

        lax.fori_loop(0, SLOTS, add_slot, jnp.zeros((CHUNK, D), F32), unroll=2)

        if c * CHUNK < FIRST:
            stage, stage_at = fetched, c * CHUNK
        else:
            stage, stage_at = fetched_end, c * CHUNK - FIRST

        def opt_tile(j, carry, at=at, stage=stage, stage_at=stage_at):
            pair = own_pair[j, at] + sums[last2[j]]
            stage[j, stage_at : stage_at + CHUNK] = finish_rows(
                opt_raw[j, at].astype(F32), backs[1, pl.ds(j, 1), :], pair
            )
            return carry

        lax.fori_loop(0, T, opt_tile, 0, unroll=2)
        rows_at = pl.ds(c * CHUNK, CHUNK)
        write = pltpu.make_async_copy(
            stage.at[pl.ds(0, T), pl.ds(stage_at, CHUNK)], opt_out.at[:, rows_at], write_sem.at[c]
        )
        write.start()
        writes.append(write)

    for turn in ORDER:
        plane_copy(turn).wait_send()
        for c in range(CHUNKS):
            back_copy(turn, 0, c).wait_send()
            back_copy(turn, 1, c).wait_send()
        back_copy(turn, 1, None).wait_send()
    for step in range(1, n_y):
        block_copy(step).wait_send()
    for y in range(n_y):
        mate_copy(y).wait_send()
    write_sar.wait()
    for write in writes:
        write.wait()


def index_tables(candidates):
    me = lax.axis_index("opt")
    block = T * GROUPS
    local_ids = (candidates % block).reshape(-1)
    hits = (local_ids[:, None] == jnp.arange(block)[None, :]).astype(jnp.int32)
    needed = jnp.max(hits, axis=0).reshape(GROUPS, T)
    rank = jnp.cumsum(needed, axis=1) - needed
    chosen = needed[:, :, None] * (rank[:, :, None] == jnp.arange(CAP)[None, None, :])
    asked = jnp.sum(chosen * jnp.arange(T)[None, :, None], axis=1)
    pair_rank = jnp.sum(hits * rank.reshape(-1)[None, :], axis=1)
    owner = local_ids // T
    turn = ((me // SIDE - owner // SIDE) % SIDE) * SIDE + (me % SIDE - owner % SIDE) % SIDE
    slot = (turn - 1) * CAP + pair_rank
    turns = jnp.arange(GROUPS)
    owners = ((me // SIDE + turns // SIDE) % SIDE) * SIDE + (me % SIDE + turns % SIDE) % SIDE
    by_turn = jnp.sum(
        (owners[:, None] == jnp.arange(GROUPS)[None, :])[:, :, None] * asked[None], axis=1
    )
    ids = jnp.zeros((GROUPS, 1, 128), jnp.int32).at[:, 0, :CAP].set(by_turn)
    pairs = jnp.arange(PAIRS)
    key = slot * 64 + pairs
    place = jnp.sum(key[None, :] < key[:, None], axis=1)
    at_place = place[None, :] == pairs[:, None]
    sorted_key = jnp.sum(at_place * key[None, :], axis=1)
    sorted_pair, sorted_slot = sorted_key % 64, sorted_key // 64
    same = (sorted_slot == jnp.concatenate([jnp.full((1,), -1), sorted_slot[:-1]])).astype(jnp.int32)
    slots = jnp.arange(SLOTS)
    upto = jnp.sum(slot[None, :] <= slots[:, None], axis=1)
    used = jnp.any(slot[None, :] == slots[:, None], axis=1)
    last = jnp.where(used, upto - 1, PAIRS)
    table = jnp.concatenate(
        [slot, sorted_pair, sorted_pair // NEG, same, last, jnp.zeros((TABLE - LAST_AT - SLOTS,))]
    )
    return table.astype(jnp.int32), ids


def per_device(n_sar, sar_tokens, opt_tokens, candidates):
    table, ids = index_tables(candidates)
    vmem = pl.BlockSpec(memory_space=pltpu.VMEM)
    dma = pltpu.SemaphoreType.DMA
    padded = jax.ShapeDtypeStruct((T, ROWS, D), BF16)
    grads = pl.pallas_call(
        functools.partial(kernel, n_sar),
        out_shape=(padded, padded),
        in_specs=[pl.BlockSpec(memory_space=pltpu.SMEM), vmem, vmem, vmem],
        out_specs=[pl.BlockSpec(memory_space=pl.ANY)] * 2,
        scratch_shapes=[
            pltpu.VMEM((T, LANES, D), BF16),
            pltpu.VMEM((T, ROWS, D), BF16),
            pltpu.VMEM((SLOTS, MAIN, D), BF16),
            pltpu.VMEM((GROUPS - 1, 16, D), BF16),
            pltpu.VMEM((SLOTS, FIRST, D), BF16),
            pltpu.VMEM((SLOTS, ROWS - FIRST, D), BF16),
            pltpu.VMEM((GROUPS - 1, 16, D), BF16),
            pltpu.VMEM((T + PAIRS, ROWS, LANES), BF16),
            pltpu.VMEM((PAIRS + 1, ROWS, HALF), BF16),
            pltpu.VMEM((ROWS, HALF), F32),
            [pltpu.VMEM((SLOTS, CHUNK, D), BF16)] * CHUNKS,
            pltpu.VMEM((GROUPS - 1, 16, D), BF16),
            pltpu.VMEM((SLOTS + 1, 8, D), F32),
            pltpu.VMEM((n_sar // 2, 2, 2, T * GROUPS, D), BF16),
            pltpu.VMEM((SLOTS + 1, CHUNK, D), F32),
            pltpu.VMEM((T, ROWS, D), F32),
            pltpu.VMEM((2, T, D), F32),
            pltpu.VMEM((2, T, D), F32),
            pltpu.VMEM((2, T, D), F32),
            pltpu.VMEM((NEG + 1, T, LANES), F32),
            pltpu.VMEM((T + PAIRS, 1, LANES), F32),
            pltpu.VMEM((16, D), F32),
            pltpu.VMEM((GROUPS, 1, 128), jnp.int32),
            pltpu.SMEM((GROUPS, 1, 128), jnp.int32),
            pltpu.SMEM((32,), jnp.int32),
            pltpu.SMEM((32,), jnp.int32),
            pltpu.SMEM((32,), jnp.int32),
            pltpu.SMEM((32,), jnp.int32),
            pltpu.SMEM((32,), jnp.int32),
            dma((GROUPS,)),
            dma((GROUPS,)),
            dma,
            dma((GROUPS, CHUNKS + 1)),
            dma((GROUPS, CHUNKS + 1)),
            dma((GROUPS, 2 * CHUNKS + 1)),
            dma((GROUPS, 2 * CHUNKS + 1)),
            dma((GROUPS,)),
            dma((GROUPS,)),
            dma((n_sar,)),
            dma((n_sar,)),
            dma((CHUNKS + 2,)),
        ],
        compiler_params=pltpu.CompilerParams(
            collective_id=0, has_side_effects=True, vmem_limit_bytes=63 * 2**20
        ),
        name="match_grads",
    )(table, ids, sar_tokens, opt_tokens)
    return tuple(grad[:, :L] for grad in grads)


def solution(mesh):
    tiles = P(("sar", "opt"), None, None)
    return jax.shard_map(
        functools.partial(per_device, mesh.shape["sar"]),
        mesh=mesh,
        in_specs=(tiles, tiles, P(("sar", "opt"), None)),
        out_specs=(tiles, tiles),
        check_vma=False,
    )
```

```python
import functools

import jax
import jax.numpy as jnp
from jax import lax
from jax.experimental import pallas as pl
from jax.experimental.pallas import tpu as pltpu
from jax.sharding import PartitionSpec as P

NEG = 3
CAP = 2
EPSILON = 1e-06
POOL_TEMP = 0.02
CAND_TEMP = 0.1
NCE_TEMP = 0.07
LOSS_SCALE = 256.0
NCE_SCALE = 0.05 * 256.0 / 0.07
LOG2E = 1.4426950408889634

T = 16
L = 196
D = 512
MAIN = 192
ROWS = 208
LANES = 256
PAIRS = T * NEG
GROUPS = 16
SIDE = 4
SLOTS = (GROUPS - 1) * CAP
CHUNK = 48
CHUNKS = MAIN // CHUNK
HALF = D // 2
FIRST = 3 * CHUNK
ORDER = [10, 2, 8, 6, 14, 9, 11, 5, 7, 13, 15, 1, 3, 4, 12]

SLOT_AT, PAIR_AT, TILE_AT, SAME_AT, LAST_AT, TABLE = 0, 48, 96, 144, 192, 256

BF16 = jnp.bfloat16
F32 = jnp.float32


def negated(turn):
    return ((SIDE - turn // SIDE) % SIDE) * SIDE + (SIDE - turn % SIDE) % SIDE


def dot(a, b, dims):
    return lax.dot_general(a, b, (dims, ((), ())), preferred_element_type=F32)


NN, NT, TN = ((1,), (0,)), ((1,), (1,)), ((0,), (0,))


def inverse_norm(rows):
    return lax.rsqrt(jnp.sum(rows * rows, axis=-1, keepdims=True) + EPSILON)


def finish_rows(raw, back, pair):
    total = pair + back
    inverse = inverse_norm(raw)
    along = jnp.sum(raw * total, axis=-1, keepdims=True)
    return ((total - raw * (inverse * inverse * along)) * inverse).astype(BF16)


def kernel(
    n_sar, table, ids, sar_in, opt_in, sar_out, opt_out,
    sar_raw, opt_raw, sar_rows, opt_rows, outbox, out_tail, fetched, fetched_end, fetched_tail, weight, parts, acc,
    returned, returned_tail, low_ends, tail_sums, pools, sums, own_pair, means, pool_rows, backs, totals,
    scale, ids_in, ids_smem, keys, ranks, order2, same2, last2,
    ids_send, ids_recv, ids_sem, fetch_send, fetch_recv, back_send, back_recv,
    plane_send, plane_recv, block_send, block_recv, write_sem, read_sem,
):
    my_sar = lax.axis_index("sar")
    me = lax.axis_index("opt")
    my_z, my_x = me // SIDE, me % SIDE

    def peer(turn):
        z = (my_z + turn // SIDE) % SIDE
        x = (my_x + turn % SIDE) % SIDE
        return {"opt": z * SIDE + x}

    n_y = n_sar // 2
    my_y, my_core = my_sar // 2, my_sar % 2

    def y_peer(step):
        return {"sar": ((my_y + step) % n_y) * 2 + my_core}

    mate = {"sar": my_y * 2 + 1 - my_core}

    def remote(src, dst, send, recv, to):
        return pltpu.make_async_remote_copy(
            src_ref=src, dst_ref=dst, send_sem=send, recv_sem=recv,
            device_id=to, device_id_type=pl.DeviceIdType.MESH,
        )

    barrier = pltpu.get_barrier_semaphore()
    for turn in range(1, GROUPS):
        pl.semaphore_signal(
            barrier, inc=1, device_id=peer(turn), device_id_type=pl.DeviceIdType.MESH
        )
    for step in range(1, n_y):
        pl.semaphore_signal(
            barrier, inc=1, device_id=y_peer(step), device_id_type=pl.DeviceIdType.MESH
        )
    pl.semaphore_signal(barrier, inc=1, device_id=mate, device_id_type=pl.DeviceIdType.MESH)

    def reads(which, source, rows):
        span = rows.shape[1]
        copies = []
        for k in range(-(-T * L // span)):
            size = min(span, T * L - k * span)
            copies.append(
                pltpu.make_async_copy(
                    source.at[pl.ds(k * span, size)],
                    rows.at[k, pl.ds(0, size)],
                    read_sem.at[which, k],
                )
            )
        return copies

    opt_reads, sar_reads = reads(1, opt_in, opt_rows), reads(0, sar_in, sar_rows)
    for copy in opt_reads + sar_reads:
        copy.start()

    def put_rows(at, values):
        for q in range(D // 128):
            own_pair[q, at] = values[:, q * 128 : (q + 1) * 128]

    def get_rows(at):
        return jnp.concatenate([own_pair[q, at] for q in range(D // 128)], axis=1)

    put_rows(pl.ds(T * L, T * (ROWS - L)), jnp.zeros((T * (ROWS - L), D), F32))

    def widen_all(copies, rows):
        span = rows.shape[1]
        for copy in copies:
            copy.wait()

        def widen(k, carry):
            put_rows(pl.ds(pl.multiple_of(k * span, 16), span), rows[k].astype(F32))
            return carry

        full = T * L // span
        rest = T * L - full * span
        lax.fori_loop(0, full, widen, 0)
        put_rows(pl.ds(full * span, rest), rows[full, 0:rest].astype(F32))

    def normalize(which, raw, rows, first, size):
        def tile(i, carry):
            values = get_rows(pl.ds(first * T + i, size, stride=T))
            unit = values * inverse_norm(values)
            raw[i, first : first + size] = values.astype(BF16)
            rows[i, first : first + size] = unit.astype(BF16)
            mean = jnp.sum(unit, axis=0, keepdims=True) * (1.0 / L)
            if first == 0:
                means[which, pl.ds(i, 1), :] = mean
            else:
                means[which, pl.ds(i, 1), :] += mean
            return carry

        lax.fori_loop(0, T, tile, 0, unroll=2)

    widen_all(opt_reads, opt_rows)

    pl.semaphore_wait(barrier, GROUPS - 1 + n_y)

    def ids_copy(turn):
        return remote(
            ids.at[turn], ids_in.at[turn], ids_send.at[turn], ids_recv.at[turn], peer(turn)
        )

    for turn in ORDER:
        ids_copy(turn).start()
    normalize(1, opt_raw, opt_rows, 0, CHUNK)
    for turn in ORDER:
        ids_copy(turn).wait()
    to_smem = pltpu.make_async_copy(ids_in, ids_smem, ids_sem)
    to_smem.start()
    to_smem.wait()

    def fetch_copy(turn, c):
        box = pl.ds((turn - 1) * CAP, CAP)
        if c == CHUNKS:
            src, dst = out_tail.at[turn - 1], fetched_tail.at[turn - 1]
        else:
            at = pl.ds(c * CHUNK, CHUNK)
            src = outbox.at[box, at]
            if c * CHUNK < FIRST:
                dst = fetched.at[box, at]
            else:
                dst = fetched_end.at[box, pl.ds(c * CHUNK - FIRST, CHUNK)]
        return remote(src, dst, fetch_send.at[turn, c], fetch_recv.at[turn, c], peer(turn))

    def pack_ends(low, high):
        upper = lax.broadcasted_iota(jnp.int32, (16, HALF), 0) % 8 < 4
        return jnp.where(upper, low, pltpu.roll(high, 4, 0)).astype(BF16)

    def unpack_ends(packed):
        upper = lax.broadcasted_iota(jnp.int32, (16, HALF), 0) % 8 < 4
        packed = packed.astype(F32)
        low = jnp.where(upper, packed, 0.0)
        high = jnp.where(upper, pltpu.roll(packed, 12, 0), 0.0)
        return jnp.concatenate([low, high], axis=1)

    def send_chunk(c):
        for turn in ORDER:
            asker = negated(turn)
            if c < CHUNKS:
                for s in range(CAP):
                    outbox[(turn - 1) * CAP + s, c * CHUNK : (c + 1) * CHUNK] = opt_rows[
                        ids_smem[asker, 0, s], c * CHUNK : (c + 1) * CHUNK
                    ]
            else:
                ends = [
                    opt_rows[ids_smem[asker, 0, s], MAIN:ROWS].astype(F32)[0:8] for s in range(CAP)
                ]
                both = jnp.concatenate(ends, axis=0)
                out_tail[turn - 1] = pack_ends(both[:, :HALF], both[:, HALF:])
            fetch_copy(turn, c).start()

    send_chunk(0)

    normalize(1, opt_raw, opt_rows, CHUNK, ROWS - CHUNK)
    widen_all(sar_reads, sar_rows)
    normalize(0, sar_raw, sar_rows, 0, ROWS)

    def clear(i, carry):
        sar_rows[i, ROWS:LANES] = jnp.zeros((LANES - ROWS, D), BF16)
        return carry

    lax.fori_loop(0, T, clear, 0)

    mine = pl.ds(pl.multiple_of(me * T, T), T)
    for which in range(2):
        mean = means[which]
        pool_scale = lax.rsqrt(jnp.sum(mean * mean, axis=-1, keepdims=True) + EPSILON)
        pool = mean * pool_scale
        pool_rows[which] = pool
        pools[my_y, my_core, which, mine, :] = pool.astype(BF16)

    def plane_copy(turn):
        here = pools.at[my_y, my_core, :, mine, :]
        return remote(here, here, plane_send.at[turn], plane_recv.at[turn], peer(turn))

    for turn in ORDER:
        plane_copy(turn).start()

    send_chunk(1)

    def exp_scores(rows, i):
        return jnp.exp2(dot(rows, sar_rows[i], NT) * (LOG2E / POOL_TEMP))

    live = lax.broadcasted_iota(jnp.int32, (ROWS, LANES), 0) < L

    def own_scores(i, carry):
        e = exp_scores(opt_rows[i], i)
        weight[i] = e.astype(BF16)
        totals[0, pl.ds(i, 1), :] = jnp.sum(jnp.where(live, e, 0.0), axis=0, keepdims=True)
        return carry

    lax.fori_loop(0, T, own_scores, 0)

    for p in range(SLOTS):
        keys[p] = ids_smem[p // CAP + 1, 0, p % CAP] * 32 + p

    def rank_of(p, carry):
        key = keys[p]
        rank = jnp.int32(0)
        for q in range(SLOTS):
            rank += (keys[q] < key).astype(jnp.int32)
        ranks[p] = rank
        return carry

    lax.fori_loop(0, SLOTS, rank_of, 0)

    def place_of(t, before):
        key = jnp.int32(0)
        for p in range(SLOTS):
            key += jnp.where(ranks[p] == t, keys[p], 0)
        tile = key // 32
        order2[t] = key % 32
        same2[t] = (tile == before).astype(jnp.int32)
        return tile

    lax.fori_loop(0, SLOTS, place_of, jnp.int32(-1))

    def last_of(j, before):
        upto = jnp.int32(0)
        for p in range(SLOTS):
            upto += (keys[p] < (j + 1) * 32).astype(jnp.int32)
        last2[j] = jnp.where(upto > before, upto - 1, SLOTS)
        return upto

    lax.fori_loop(0, T, last_of, jnp.int32(0))

    for turn in ORDER:
        plane_copy(turn).wait_recv()

    def block_copy(step):
        here = pools.at[my_y, my_core]
        return remote(here, here, block_send.at[step], block_recv.at[step], y_peer(step))

    def mate_copy(y):
        here = pools.at[y, my_core]
        return remote(here, here, block_send.at[n_y + y], block_recv.at[n_y + y], mate)

    for step in range(1, n_y):
        block_copy(step).start()
        if step + 1 < CHUNKS:
            send_chunk(step + 1)
    for c in range(n_y, CHUNKS + 1):
        send_chunk(c)

    for c in range(FIRST // CHUNK):
        for turn in ORDER:
            fetch_copy(turn, c).wait_recv()

    def first_scores(i, carry):
        rows = [fetched[table[SLOT_AT + i * NEG + k]] for k in range(NEG)]
        exps = exp_scores(jnp.concatenate(rows, axis=0), i)
        for k in range(NEG):
            e = exps[k * FIRST : (k + 1) * FIRST]
            weight[T + i * NEG + k, 0:FIRST] = e.astype(BF16)
            totals[k + 1, pl.ds(i, 1), :] = jnp.sum(e, axis=0, keepdims=True)
        return carry

    lax.fori_loop(0, T, first_scores, 0)

    for c in range(FIRST // CHUNK, CHUNKS + 1):
        for turn in ORDER:
            fetch_copy(turn, c).wait_recv()
    for turn in range(1, GROUPS):
        ends = unpack_ends(fetched_tail[turn - 1])
        for s in range(CAP):
            end = ends[8 * s : 8 * s + 8]
            fetched_end[(turn - 1) * CAP + s, MAIN - FIRST :] = jnp.concatenate(
                [end, jnp.zeros_like(end)], axis=0
            ).astype(BF16)

    live_end = lax.broadcasted_iota(jnp.int32, (ROWS - FIRST, LANES), 0) < L - FIRST

    def last_scores(i, carry):
        rows = [fetched_end[table[SLOT_AT + i * NEG + k]] for k in range(NEG)]
        exps = exp_scores(jnp.concatenate(rows, axis=0), i)
        for k in range(NEG):
            e = exps[k * (ROWS - FIRST) : (k + 1) * (ROWS - FIRST)]
            weight[T + i * NEG + k, FIRST:ROWS] = e.astype(BF16)
            totals[k + 1, pl.ds(i, 1), :] += jnp.sum(
                jnp.where(live_end, e, 0.0), axis=0, keepdims=True
            )
        return carry

    lax.fori_loop(0, T, last_scores, 0, unroll=2)

    for step in range(1, n_y):
        block_copy(step).wait_recv()
    for y in range(n_y):
        mate_copy(y).start()

    tokens = lax.broadcasted_iota(jnp.int32, (T, LANES), 1) < L
    cand = []
    for k in range(NEG + 1):
        logs = jnp.where(tokens, jnp.log(totals[k]), 0.0)
        match = (POOL_TEMP / L) * jnp.sum(logs, axis=-1, keepdims=True)
        cand.append(jnp.exp(match / CAND_TEMP))
    cand_sum = cand[0] + cand[1] + cand[2] + cand[3]
    for k in range(NEG + 1):
        coef = LOSS_SCALE * (cand[k] / cand_sum - (1.0 if k == 0 else 0.0)) / CAND_TEMP
        scaled = (coef / L) / totals[k]
        for i in range(T):
            scale[i if k == 0 else T + i * NEG + k - 1] = scaled[i : i + 1]

    def weights(p):
        return (weight[p].astype(F32) * scale[p]).astype(BF16)

    def back_copy(turn, h, c):
        box = pl.ds((turn - 1) * CAP, CAP)
        if c is None:
            src, dst = out_tail.at[turn - 1], returned_tail.at[turn - 1]
            sem = 2 * CHUNKS
        else:
            at, cols = pl.ds(c * CHUNK, CHUNK), pl.ds(h * HALF, HALF)
            src, dst = outbox.at[box, at, cols], returned[c].at[box, :, cols]
            sem = h * CHUNKS + c
        return remote(src, dst, back_send.at[turn, sem], back_recv.at[turn, sem], peer(turn))

    parts[PAIRS] = jnp.zeros((ROWS, HALF), BF16)
    for c in range(CHUNKS + 1):
        for turn in ORDER:
            fetch_copy(turn, c).wait_send()
    for h in range(2):
        cols = slice(h * HALF, (h + 1) * HALF)
        acc[...] = jnp.zeros_like(acc)

        def add_pair(p, carry, cols=cols):
            pair = table[PAIR_AT + p]
            keep = table[SAME_AT + p].astype(F32)
            part = dot(weights(T + pair), sar_rows[table[TILE_AT + p], :, cols], NN)
            total = acc[...] * keep + part
            acc[...] = total
            parts[p] = total.astype(BF16)
            return carry

        lax.fori_loop(0, PAIRS, add_pair, 0, unroll=2)

        def send_tails(h=h, cols=cols):
            for turn in ORDER:
                ends = [
                    parts[table[LAST_AT + (negated(turn) - 1) * CAP + s], MAIN:ROWS].astype(F32)[0:8]
                    for s in range(CAP)
                ]
                both = jnp.concatenate(ends, axis=0)
                if h:
                    out_tail[turn - 1] = pack_ends(low_ends[turn - 1], both)
                    back_copy(turn, h, None).start()
                else:
                    low_ends[turn - 1] = both

        if h:
            send_tails()
        for c in range(CHUNKS):
            at = slice(c * CHUNK, (c + 1) * CHUNK)
            for turn in ORDER:
                for s in range(CAP):
                    last = table[LAST_AT + (negated(turn) - 1) * CAP + s]
                    outbox[(turn - 1) * CAP + s, at, cols] = parts[last, at, :]
                back_copy(turn, h, c).start()
        if not h:
            send_tails()

    for y in range(n_y):
        mate_copy(y).wait_recv()
    block = pools.shape[3]
    logit_scale = LOG2E / NCE_TEMP
    own_sar = pools[my_y, my_core, 0, mine, :]
    own_opt = pools[my_y, my_core, 1, mine, :]

    def own_rows(t, row_sums):
        e = jnp.exp2(dot(own_sar, pools[t // 2, t % 2, 1], NT) * logit_scale)
        return row_sums + jnp.sum(e, axis=-1, keepdims=True)

    row_sums = lax.fori_loop(0, n_sar, own_rows, jnp.zeros((T, 1), F32))

    def own_coefs(t, grad):
        e = jnp.exp2(dot(own_sar, pools[t // 2, t % 2, 1], NT) * logit_scale)
        rows = my_sar * block + me * T + lax.broadcasted_iota(jnp.int32, (T, block), 0)
        columns = t * block + lax.broadcasted_iota(jnp.int32, (T, block), 1)
        diagonal = (rows == columns).astype(F32)
        coefs = (NCE_SCALE * (e / row_sums - diagonal)).astype(BF16)
        return grad + dot(coefs, pools[t // 2, t % 2, 1], NN)

    sar_pool_grad = lax.fori_loop(0, n_sar, own_coefs, jnp.zeros((T, D), F32))

    def opt_coefs(s, grad):
        rows_here = pools[s // 2, s % 2, 0]

        def add_sums(t, sums_here):
            e = jnp.exp2(dot(rows_here, pools[t // 2, t % 2, 1], NT) * logit_scale)
            return sums_here + jnp.sum(e, axis=-1, keepdims=True)

        sums_here = lax.fori_loop(0, n_sar, add_sums, jnp.zeros((block, 1), F32))
        e = jnp.exp2(dot(rows_here, own_opt, NT) * logit_scale)
        rows = s * block + lax.broadcasted_iota(jnp.int32, (block, T), 0)
        columns = my_sar * block + me * T + lax.broadcasted_iota(jnp.int32, (block, T), 1)
        diagonal = (rows == columns).astype(F32)
        coefs = (NCE_SCALE * (e / sums_here - diagonal)).astype(BF16)
        return grad + dot(coefs, rows_here, TN)

    opt_pool_grad = lax.fori_loop(0, n_sar, opt_coefs, jnp.zeros((T, D), F32))

    for which, grad in enumerate((sar_pool_grad, opt_pool_grad)):
        mean = means[which]
        pool_scale = lax.rsqrt(jnp.sum(mean * mean, axis=-1, keepdims=True) + EPSILON)
        pool = pool_rows[which]
        along = jnp.sum(pool * grad, axis=-1, keepdims=True)
        backs[which] = (grad - pool * along) * pool_scale * (1.0 / L)

    def own_at(i, size=ROWS, first=0):
        return pl.ds(pl.multiple_of(i * ROWS + first, 16), size)

    def sar_tile(i, carry):
        own = weights(i)
        put_rows(own_at(i), dot(own, sar_rows[i], NN))
        cands = [opt_rows[i]]
        coefs = [own]
        for k in range(NEG):
            cands.append(fetched[table[SLOT_AT + i * NEG + k]])
            cands.append(fetched_end[table[SLOT_AT + i * NEG + k]])
            coefs.append(weights(T + i * NEG + k))
        pair = dot(jnp.concatenate(coefs, axis=0), jnp.concatenate(cands, axis=0), TN)
        back = backs[0, pl.ds(i, 1), :]
        opt_rows[i] = finish_rows(sar_raw[i].astype(F32), back, pair[0:ROWS])
        return carry

    lax.fori_loop(0, T, sar_tile, 0)
    write_sar = pltpu.make_async_copy(opt_rows, sar_out, write_sem.at[CHUNKS + 1])
    write_sar.start()

    sums[SLOTS] = jnp.zeros((CHUNK, D), F32)
    tail_sums[SLOTS] = jnp.zeros((8, D), F32)
    writes = []
    for turn in ORDER:
        back_copy(turn, 1, None).wait_recv()

    def add_tail(t, total):
        place = order2[t]
        both = unpack_ends(returned_tail[place // CAP])
        second = (place % CAP).astype(F32)
        total = total * same2[t].astype(F32) + both[0:8] * (1.0 - second) + both[8:16] * second
        tail_sums[t] = total
        return total

    lax.fori_loop(0, SLOTS, add_tail, jnp.zeros((8, D), F32))

    def opt_tail(j, carry):
        part = tail_sums[last2[j]]
        pair = get_rows(own_at(j, ROWS - MAIN, MAIN)) + jnp.concatenate([part, jnp.zeros_like(part)], axis=0)
        fetched_end[j, MAIN - FIRST :] = finish_rows(
            opt_raw[j, MAIN:ROWS].astype(F32), backs[1, pl.ds(j, 1), :], pair
        )
        return carry

    lax.fori_loop(0, T, opt_tail, 0)
    rows_at = pl.ds(MAIN, ROWS - MAIN)
    write = pltpu.make_async_copy(
        fetched_end.at[pl.ds(0, T), pl.ds(MAIN - FIRST, ROWS - MAIN)],
        opt_out.at[:, rows_at],
        write_sem.at[CHUNKS],
    )
    write.start()
    writes.append(write)

    for c in range(CHUNKS):
        at = slice(c * CHUNK, (c + 1) * CHUNK)
        for turn in ORDER:
            back_copy(turn, 0, c).wait_recv()
            back_copy(turn, 1, c).wait_recv()

        def add_slot(t, total, c=c):
            total = total * same2[t].astype(F32) + returned[c][order2[t]].astype(F32)
            sums[t] = total
            return total

        lax.fori_loop(0, SLOTS, add_slot, jnp.zeros((CHUNK, D), F32), unroll=2)

        if c * CHUNK < FIRST:
            stage, stage_at = fetched, c * CHUNK
        else:
            stage, stage_at = fetched_end, c * CHUNK - FIRST

        def opt_tile(j, carry, c=c, at=at, stage=stage, stage_at=stage_at):
            pair = get_rows(own_at(j, CHUNK, c * CHUNK)) + sums[last2[j]]
            stage[j, stage_at : stage_at + CHUNK] = finish_rows(
                opt_raw[j, at].astype(F32), backs[1, pl.ds(j, 1), :], pair
            )
            return carry

        lax.fori_loop(0, T, opt_tile, 0, unroll=2)
        rows_at = pl.ds(c * CHUNK, CHUNK)
        write = pltpu.make_async_copy(
            stage.at[pl.ds(0, T), pl.ds(stage_at, CHUNK)], opt_out.at[:, rows_at], write_sem.at[c]
        )
        write.start()
        writes.append(write)

    for turn in ORDER:
        plane_copy(turn).wait_send()
        for c in range(CHUNKS):
            back_copy(turn, 0, c).wait_send()
            back_copy(turn, 1, c).wait_send()
        back_copy(turn, 1, None).wait_send()
    for step in range(1, n_y):
        block_copy(step).wait_send()
    for y in range(n_y):
        mate_copy(y).wait_send()
    write_sar.wait()
    for write in writes:
        write.wait()


def index_tables(candidates):
    me = lax.axis_index("opt")
    block = T * GROUPS
    local_ids = (candidates % block).reshape(-1)
    hits = (local_ids[:, None] == jnp.arange(block)[None, :]).astype(jnp.int32)
    needed = jnp.max(hits, axis=0).reshape(GROUPS, T)
    rank = jnp.cumsum(needed, axis=1) - needed
    chosen = needed[:, :, None] * (rank[:, :, None] == jnp.arange(CAP)[None, None, :])
    asked = jnp.sum(chosen * jnp.arange(T)[None, :, None], axis=1)
    pair_rank = jnp.sum(hits * rank.reshape(-1)[None, :], axis=1)
    owner = local_ids // T
    turn = ((me // SIDE - owner // SIDE) % SIDE) * SIDE + (me % SIDE - owner % SIDE) % SIDE
    slot = (turn - 1) * CAP + pair_rank
    turns = jnp.arange(GROUPS)
    owners = ((me // SIDE + turns // SIDE) % SIDE) * SIDE + (me % SIDE + turns % SIDE) % SIDE
    by_turn = jnp.sum(
        (owners[:, None] == jnp.arange(GROUPS)[None, :])[:, :, None] * asked[None], axis=1
    )
    ids = jnp.zeros((GROUPS, 1, 128), jnp.int32).at[:, 0, :CAP].set(by_turn)
    pairs = jnp.arange(PAIRS)
    key = slot * 64 + pairs
    place = jnp.sum(key[None, :] < key[:, None], axis=1)
    at_place = place[None, :] == pairs[:, None]
    sorted_key = jnp.sum(at_place * key[None, :], axis=1)
    sorted_pair, sorted_slot = sorted_key % 64, sorted_key // 64
    same = (sorted_slot == jnp.concatenate([jnp.full((1,), -1), sorted_slot[:-1]])).astype(jnp.int32)
    slots = jnp.arange(SLOTS)
    upto = jnp.sum(slot[None, :] <= slots[:, None], axis=1)
    used = jnp.any(slot[None, :] == slots[:, None], axis=1)
    last = jnp.where(used, upto - 1, PAIRS)
    table = jnp.concatenate(
        [slot, sorted_pair, sorted_pair // NEG, same, last, jnp.zeros((TABLE - LAST_AT - SLOTS,))]
    )
    return table.astype(jnp.int32), ids


def by_token(tokens):
    return jnp.swapaxes(tokens, 0, 1).reshape(-1, D)


def per_device(n_sar, sar_tokens, opt_tokens, candidates):
    table, ids = index_tables(candidates)
    vmem = pl.BlockSpec(memory_space=pltpu.VMEM)
    hbm = pl.BlockSpec(memory_space=pl.ANY)
    dma = pltpu.SemaphoreType.DMA
    padded = jax.ShapeDtypeStruct((T, ROWS, D), BF16)
    grads = pl.pallas_call(
        functools.partial(kernel, n_sar),
        out_shape=(padded, padded),
        in_specs=[pl.BlockSpec(memory_space=pltpu.SMEM), vmem, hbm, hbm],
        out_specs=[hbm] * 2,
        scratch_shapes=[
            pltpu.VMEM((T, ROWS, D), BF16),
            pltpu.VMEM((T, ROWS, D), BF16),
            pltpu.VMEM((T, LANES, D), BF16),
            pltpu.VMEM((T, ROWS, D), BF16),
            pltpu.VMEM((SLOTS, MAIN, D), BF16),
            pltpu.VMEM((GROUPS - 1, 16, HALF), BF16),
            pltpu.VMEM((SLOTS, FIRST, D), BF16),
            pltpu.VMEM((SLOTS, ROWS - FIRST, D), BF16),
            pltpu.VMEM((GROUPS - 1, 16, HALF), BF16),
            pltpu.VMEM((T + PAIRS, ROWS, LANES), BF16),
            pltpu.VMEM((PAIRS + 1, ROWS, HALF), BF16),
            pltpu.VMEM((ROWS, HALF), F32),
            [pltpu.VMEM((SLOTS, CHUNK, D), BF16)] * CHUNKS,
            pltpu.VMEM((GROUPS - 1, 16, HALF), BF16),
            pltpu.VMEM((GROUPS - 1, 16, HALF), F32),
            pltpu.VMEM((SLOTS + 1, 8, D), F32),
            pltpu.VMEM((n_sar // 2, 2, 2, T * GROUPS, D), BF16),
            pltpu.VMEM((SLOTS + 1, CHUNK, D), F32),
            pltpu.VMEM((D // 128, T * ROWS, 128), F32),
            pltpu.VMEM((2, T, D), F32),
            pltpu.VMEM((2, T, D), F32),
            pltpu.VMEM((2, T, D), F32),
            pltpu.VMEM((NEG + 1, T, LANES), F32),
            pltpu.VMEM((T + PAIRS, 1, LANES), F32),
            pltpu.VMEM((GROUPS, 1, 128), jnp.int32),
            pltpu.SMEM((GROUPS, 1, 128), jnp.int32),
            pltpu.SMEM((32,), jnp.int32),
            pltpu.SMEM((32,), jnp.int32),
            pltpu.SMEM((32,), jnp.int32),
            pltpu.SMEM((32,), jnp.int32),
            pltpu.SMEM((32,), jnp.int32),
            dma((GROUPS,)),
            dma((GROUPS,)),
            dma,
            dma((GROUPS, CHUNKS + 1)),
            dma((GROUPS, CHUNKS + 1)),
            dma((GROUPS, 2 * CHUNKS + 1)),
            dma((GROUPS, 2 * CHUNKS + 1)),
            dma((GROUPS,)),
            dma((GROUPS,)),
            dma((n_sar,)),
            dma((n_sar,)),
            dma((CHUNKS + 2,)),
            dma((2, T)),
        ],
        compiler_params=pltpu.CompilerParams(
            collective_id=0, has_side_effects=True, vmem_limit_bytes=63 * 2**20
        ),
        name="match_grads",
    )(table, ids, by_token(sar_tokens), by_token(opt_tokens))
    return tuple(grad[:, :L] for grad in grads)


def solution(mesh):
    tiles = P(("sar", "opt"), None, None)
    return jax.shard_map(
        functools.partial(per_device, mesh.shape["sar"]),
        mesh=mesh,
        in_specs=(tiles, tiles, P(("sar", "opt"), None)),
        out_specs=(tiles, tiles),
        check_vma=False,
    )
```

```python
import functools

import jax
import jax.numpy as jnp
from jax import lax
from jax.experimental import pallas as pl
from jax.experimental.pallas import tpu as pltpu
from jax.sharding import PartitionSpec as P

NEG = 3
CAP = 2
EPSILON = 1e-06
POOL_TEMP = 0.02
CAND_TEMP = 0.1
NCE_TEMP = 0.07
LOSS_SCALE = 256.0
NCE_SCALE = 0.05 * 256.0 / 0.07
LOG2E = 1.4426950408889634

T = 16
L = 196
D = 512
MAIN = 192
ROWS = 208
LANES = 256
PAIRS = T * NEG
GROUPS = 16
SIDE = 4
SLOTS = (GROUPS - 1) * CAP
CHUNK = 48
CHUNKS = MAIN // CHUNK
HALF = D // 2
FIRST = 3 * CHUNK
ORDER = [10, 2, 8, 6, 14, 9, 11, 5, 7, 13, 15, 1, 3, 4, 12]

SLOT_AT, PAIR_AT, TILE_AT, SAME_AT, LAST_AT, TABLE = 0, 48, 96, 144, 192, 256

BF16 = jnp.bfloat16
F32 = jnp.float32


def negated(turn):
    return ((SIDE - turn // SIDE) % SIDE) * SIDE + (SIDE - turn % SIDE) % SIDE


def dot(a, b, dims):
    return lax.dot_general(a, b, (dims, ((), ())), preferred_element_type=F32)


NN, NT, TN = ((1,), (0,)), ((1,), (1,)), ((0,), (0,))


def inverse_norm(rows):
    return lax.rsqrt(jnp.sum(rows * rows, axis=-1, keepdims=True) + EPSILON)


def finish_rows(raw, back, pair):
    total = pair + back
    inverse = inverse_norm(raw)
    along = jnp.sum(raw * total, axis=-1, keepdims=True)
    return (total - raw * (inverse * inverse * along)) * inverse


def kernel(
    n_sar, table, ids, sar_in, opt_in, sar_out, opt_out,
    sar_raw, opt_raw, sar_rows, opt_rows, outbox, out_tail, fetched, fetched_end, fetched_tail, weight, parts, acc,
    returned, returned_tail, low_ends, tail_sums, pools, sums, own_pair, means, pool_rows, backs, totals,
    scale, by_row, staged, ids_in, ids_smem, keys, ranks, order2, same2, last2,
    ids_send, ids_recv, ids_sem, fetch_send, fetch_recv, back_send, back_recv,
    plane_send, plane_recv, block_send, block_recv, write_sem, read_sem,
):
    my_sar = lax.axis_index("sar")
    me = lax.axis_index("opt")
    my_z, my_x = me // SIDE, me % SIDE

    def peer(turn):
        z = (my_z + turn // SIDE) % SIDE
        x = (my_x + turn % SIDE) % SIDE
        return {"opt": z * SIDE + x}

    n_y = n_sar // 2
    my_y, my_core = my_sar // 2, my_sar % 2

    def y_peer(step):
        return {"sar": ((my_y + step) % n_y) * 2 + my_core}

    mate = {"sar": my_y * 2 + 1 - my_core}

    def remote(src, dst, send, recv, to):
        return pltpu.make_async_remote_copy(
            src_ref=src, dst_ref=dst, send_sem=send, recv_sem=recv,
            device_id=to, device_id_type=pl.DeviceIdType.MESH,
        )

    barrier = pltpu.get_barrier_semaphore()
    for turn in range(1, GROUPS):
        pl.semaphore_signal(
            barrier, inc=1, device_id=peer(turn), device_id_type=pl.DeviceIdType.MESH
        )
    for step in range(1, n_y):
        pl.semaphore_signal(
            barrier, inc=1, device_id=y_peer(step), device_id_type=pl.DeviceIdType.MESH
        )
    pl.semaphore_signal(barrier, inc=1, device_id=mate, device_id_type=pl.DeviceIdType.MESH)

    def reads(which, source, rows):
        span = rows.shape[1]
        copies = []
        for k in range(-(-T * L // span)):
            size = min(span, T * L - k * span)
            copies.append(
                pltpu.make_async_copy(
                    source.at[pl.ds(k * span, size)],
                    rows.at[k, pl.ds(0, size)],
                    read_sem.at[which, k],
                )
            )
        return copies

    opt_reads, sar_reads = reads(1, opt_in, opt_rows), reads(0, sar_in, sar_rows)
    for copy in opt_reads + sar_reads:
        copy.start()

    def put_rows(at, values):
        for q in range(D // 128):
            own_pair[q, at] = values[:, q * 128 : (q + 1) * 128]

    def get_rows(at):
        return jnp.concatenate([own_pair[q, at] for q in range(D // 128)], axis=1)

    put_rows(pl.ds(T * L, T * (ROWS - L)), jnp.zeros((T * (ROWS - L), D), F32))

    def widen_all(copies, rows):
        span = rows.shape[1]
        for copy in copies:
            copy.wait()

        def widen(k, carry):
            put_rows(pl.ds(pl.multiple_of(k * span, 16), span), rows[k].astype(F32))
            return carry

        full = T * L // span
        rest = T * L - full * span
        lax.fori_loop(0, full, widen, 0)
        put_rows(pl.ds(full * span, rest), rows[full, 0:rest].astype(F32))

    def normalize(which, raw, rows, first, size):
        def tile(i, carry):
            values = get_rows(pl.ds(first * T + i, size, stride=T))
            unit = values * inverse_norm(values)
            raw[i, first : first + size] = values.astype(BF16)
            rows[i, first : first + size] = unit.astype(BF16)
            mean = jnp.sum(unit, axis=0, keepdims=True) * (1.0 / L)
            if first == 0:
                means[which, pl.ds(i, 1), :] = mean
            else:
                means[which, pl.ds(i, 1), :] += mean
            return carry

        lax.fori_loop(0, T, tile, 0, unroll=2)

    widen_all(opt_reads, opt_rows)

    pl.semaphore_wait(barrier, GROUPS - 1 + n_y)

    def ids_copy(turn):
        return remote(
            ids.at[turn], ids_in.at[turn], ids_send.at[turn], ids_recv.at[turn], peer(turn)
        )

    for turn in ORDER:
        ids_copy(turn).start()
    normalize(1, opt_raw, opt_rows, 0, CHUNK)
    for turn in ORDER:
        ids_copy(turn).wait()
    to_smem = pltpu.make_async_copy(ids_in, ids_smem, ids_sem)
    to_smem.start()
    to_smem.wait()

    def fetch_copy(turn, c):
        box = pl.ds((turn - 1) * CAP, CAP)
        if c == CHUNKS:
            src, dst = out_tail.at[turn - 1], fetched_tail.at[turn - 1]
        else:
            at = pl.ds(c * CHUNK, CHUNK)
            src = outbox.at[box, at]
            if c * CHUNK < FIRST:
                dst = fetched.at[box, at]
            else:
                dst = fetched_end.at[box, pl.ds(c * CHUNK - FIRST, CHUNK)]
        return remote(src, dst, fetch_send.at[turn, c], fetch_recv.at[turn, c], peer(turn))

    def pack_ends(low, high):
        upper = lax.broadcasted_iota(jnp.int32, (16, HALF), 0) % 8 < 4
        return jnp.where(upper, low, pltpu.roll(high, 4, 0)).astype(BF16)

    def unpack_ends(packed):
        upper = lax.broadcasted_iota(jnp.int32, (16, HALF), 0) % 8 < 4
        packed = packed.astype(F32)
        low = jnp.where(upper, packed, 0.0)
        high = jnp.where(upper, pltpu.roll(packed, 12, 0), 0.0)
        return jnp.concatenate([low, high], axis=1)

    def send_chunk(c):
        for turn in ORDER:
            asker = negated(turn)
            if c < CHUNKS:
                for s in range(CAP):
                    outbox[(turn - 1) * CAP + s, c * CHUNK : (c + 1) * CHUNK] = opt_rows[
                        ids_smem[asker, 0, s], c * CHUNK : (c + 1) * CHUNK
                    ]
            else:
                ends = [
                    opt_rows[ids_smem[asker, 0, s], MAIN:ROWS].astype(F32)[0:8] for s in range(CAP)
                ]
                both = jnp.concatenate(ends, axis=0)
                out_tail[turn - 1] = pack_ends(both[:, :HALF], both[:, HALF:])
            fetch_copy(turn, c).start()

    send_chunk(0)

    normalize(1, opt_raw, opt_rows, CHUNK, ROWS - CHUNK)
    widen_all(sar_reads, sar_rows)
    normalize(0, sar_raw, sar_rows, 0, ROWS)

    def clear(i, carry):
        sar_rows[i, ROWS:LANES] = jnp.zeros((LANES - ROWS, D), BF16)
        return carry

    lax.fori_loop(0, T, clear, 0)

    mine = pl.ds(pl.multiple_of(me * T, T), T)
    for which in range(2):
        mean = means[which]
        pool_scale = lax.rsqrt(jnp.sum(mean * mean, axis=-1, keepdims=True) + EPSILON)
        pool = mean * pool_scale
        pool_rows[which] = pool
        pools[my_y, my_core, which, mine, :] = pool.astype(BF16)

    def plane_copy(turn):
        here = pools.at[my_y, my_core, :, mine, :]
        return remote(here, here, plane_send.at[turn], plane_recv.at[turn], peer(turn))

    for turn in ORDER:
        plane_copy(turn).start()

    send_chunk(1)

    def exp_scores(rows, i):
        return jnp.exp2(dot(rows, sar_rows[i], NT) * (LOG2E / POOL_TEMP))

    live = lax.broadcasted_iota(jnp.int32, (ROWS, LANES), 0) < L

    def own_scores(i, carry):
        e = exp_scores(opt_rows[i], i)
        weight[i] = e.astype(BF16)
        totals[0, pl.ds(i, 1), :] = jnp.sum(jnp.where(live, e, 0.0), axis=0, keepdims=True)
        return carry

    lax.fori_loop(0, T, own_scores, 0)

    for p in range(SLOTS):
        keys[p] = ids_smem[p // CAP + 1, 0, p % CAP] * 32 + p

    def rank_of(p, carry):
        key = keys[p]
        rank = jnp.int32(0)
        for q in range(SLOTS):
            rank += (keys[q] < key).astype(jnp.int32)
        ranks[p] = rank
        return carry

    lax.fori_loop(0, SLOTS, rank_of, 0)

    def place_of(t, before):
        key = jnp.int32(0)
        for p in range(SLOTS):
            key += jnp.where(ranks[p] == t, keys[p], 0)
        tile = key // 32
        order2[t] = key % 32
        same2[t] = (tile == before).astype(jnp.int32)
        return tile

    lax.fori_loop(0, SLOTS, place_of, jnp.int32(-1))

    def last_of(j, before):
        upto = jnp.int32(0)
        for p in range(SLOTS):
            upto += (keys[p] < (j + 1) * 32).astype(jnp.int32)
        last2[j] = jnp.where(upto > before, upto - 1, SLOTS)
        return upto

    lax.fori_loop(0, T, last_of, jnp.int32(0))

    for turn in ORDER:
        plane_copy(turn).wait_recv()

    def block_copy(step):
        here = pools.at[my_y, my_core]
        return remote(here, here, block_send.at[step], block_recv.at[step], y_peer(step))

    def mate_copy(y):
        here = pools.at[y, my_core]
        return remote(here, here, block_send.at[n_y + y], block_recv.at[n_y + y], mate)

    for step in range(1, n_y):
        block_copy(step).start()
        if step + 1 < CHUNKS:
            send_chunk(step + 1)
    for c in range(n_y, CHUNKS + 1):
        send_chunk(c)

    for c in range(FIRST // CHUNK):
        for turn in ORDER:
            fetch_copy(turn, c).wait_recv()

    def first_scores(i, carry):
        rows = [fetched[table[SLOT_AT + i * NEG + k]] for k in range(NEG)]
        exps = exp_scores(jnp.concatenate(rows, axis=0), i)
        for k in range(NEG):
            e = exps[k * FIRST : (k + 1) * FIRST]
            weight[T + i * NEG + k, 0:FIRST] = e.astype(BF16)
            totals[k + 1, pl.ds(i, 1), :] = jnp.sum(e, axis=0, keepdims=True)
        return carry

    lax.fori_loop(0, T, first_scores, 0)

    for c in range(FIRST // CHUNK, CHUNKS + 1):
        for turn in ORDER:
            fetch_copy(turn, c).wait_recv()
    for turn in range(1, GROUPS):
        ends = unpack_ends(fetched_tail[turn - 1])
        for s in range(CAP):
            end = ends[8 * s : 8 * s + 8]
            fetched_end[(turn - 1) * CAP + s, MAIN - FIRST :] = jnp.concatenate(
                [end, jnp.zeros_like(end)], axis=0
            ).astype(BF16)

    live_end = lax.broadcasted_iota(jnp.int32, (ROWS - FIRST, LANES), 0) < L - FIRST

    def last_scores(i, carry):
        rows = [fetched_end[table[SLOT_AT + i * NEG + k]] for k in range(NEG)]
        exps = exp_scores(jnp.concatenate(rows, axis=0), i)
        for k in range(NEG):
            e = exps[k * (ROWS - FIRST) : (k + 1) * (ROWS - FIRST)]
            weight[T + i * NEG + k, FIRST:ROWS] = e.astype(BF16)
            totals[k + 1, pl.ds(i, 1), :] += jnp.sum(
                jnp.where(live_end, e, 0.0), axis=0, keepdims=True
            )
        return carry

    lax.fori_loop(0, T, last_scores, 0, unroll=2)

    for step in range(1, n_y):
        block_copy(step).wait_recv()
    for y in range(n_y):
        mate_copy(y).start()

    tokens = lax.broadcasted_iota(jnp.int32, (T, LANES), 1) < L
    cand = []
    for k in range(NEG + 1):
        logs = jnp.where(tokens, jnp.log(totals[k]), 0.0)
        match = (POOL_TEMP / L) * jnp.sum(logs, axis=-1, keepdims=True)
        cand.append(jnp.exp(match / CAND_TEMP))
    cand_sum = cand[0] + cand[1] + cand[2] + cand[3]
    for k in range(NEG + 1):
        coef = LOSS_SCALE * (cand[k] / cand_sum - (1.0 if k == 0 else 0.0)) / CAND_TEMP
        scaled = (coef / L) / totals[k]
        for i in range(T):
            scale[i if k == 0 else T + i * NEG + k - 1] = scaled[i : i + 1]

    def weights(p):
        return (weight[p].astype(F32) * scale[p]).astype(BF16)

    def back_copy(turn, h, c):
        box = pl.ds((turn - 1) * CAP, CAP)
        if c is None:
            src, dst = out_tail.at[turn - 1], returned_tail.at[turn - 1]
            sem = 2 * CHUNKS
        else:
            at, cols = pl.ds(c * CHUNK, CHUNK), pl.ds(h * HALF, HALF)
            src, dst = outbox.at[box, at, cols], returned[c].at[box, :, cols]
            sem = h * CHUNKS + c
        return remote(src, dst, back_send.at[turn, sem], back_recv.at[turn, sem], peer(turn))

    parts[PAIRS] = jnp.zeros((ROWS, HALF), BF16)
    for c in range(CHUNKS + 1):
        for turn in ORDER:
            fetch_copy(turn, c).wait_send()
    for h in range(2):
        cols = slice(h * HALF, (h + 1) * HALF)
        acc[...] = jnp.zeros_like(acc)

        def add_pair(p, carry, cols=cols):
            pair = table[PAIR_AT + p]
            keep = table[SAME_AT + p].astype(F32)
            part = dot(weights(T + pair), sar_rows[table[TILE_AT + p], :, cols], NN)
            total = acc[...] * keep + part
            acc[...] = total
            parts[p] = total.astype(BF16)
            return carry

        lax.fori_loop(0, PAIRS, add_pair, 0, unroll=2)

        def send_tails(h=h, cols=cols):
            for turn in ORDER:
                ends = [
                    parts[table[LAST_AT + (negated(turn) - 1) * CAP + s], MAIN:ROWS].astype(F32)[0:8]
                    for s in range(CAP)
                ]
                both = jnp.concatenate(ends, axis=0)
                if h:
                    out_tail[turn - 1] = pack_ends(low_ends[turn - 1], both)
                    back_copy(turn, h, None).start()
                else:
                    low_ends[turn - 1] = both

        if h:
            send_tails()
        for c in range(CHUNKS):
            at = slice(c * CHUNK, (c + 1) * CHUNK)
            for turn in ORDER:
                for s in range(CAP):
                    last = table[LAST_AT + (negated(turn) - 1) * CAP + s]
                    outbox[(turn - 1) * CAP + s, at, cols] = parts[last, at, :]
                back_copy(turn, h, c).start()
        if not h:
            send_tails()

    for y in range(n_y):
        mate_copy(y).wait_recv()
    block = pools.shape[3]
    logit_scale = LOG2E / NCE_TEMP
    own_sar = pools[my_y, my_core, 0, mine, :]
    own_opt = pools[my_y, my_core, 1, mine, :]

    def own_rows(t, row_sums):
        e = jnp.exp2(dot(own_sar, pools[t // 2, t % 2, 1], NT) * logit_scale)
        return row_sums + jnp.sum(e, axis=-1, keepdims=True)

    row_sums = lax.fori_loop(0, n_sar, own_rows, jnp.zeros((T, 1), F32))

    def own_coefs(t, grad):
        e = jnp.exp2(dot(own_sar, pools[t // 2, t % 2, 1], NT) * logit_scale)
        rows = my_sar * block + me * T + lax.broadcasted_iota(jnp.int32, (T, block), 0)
        columns = t * block + lax.broadcasted_iota(jnp.int32, (T, block), 1)
        diagonal = (rows == columns).astype(F32)
        coefs = (NCE_SCALE * (e / row_sums - diagonal)).astype(BF16)
        return grad + dot(coefs, pools[t // 2, t % 2, 1], NN)

    sar_pool_grad = lax.fori_loop(0, n_sar, own_coefs, jnp.zeros((T, D), F32))

    def opt_coefs(s, grad):
        rows_here = pools[s // 2, s % 2, 0]

        def add_sums(t, sums_here):
            e = jnp.exp2(dot(rows_here, pools[t // 2, t % 2, 1], NT) * logit_scale)
            return sums_here + jnp.sum(e, axis=-1, keepdims=True)

        sums_here = lax.fori_loop(0, n_sar, add_sums, jnp.zeros((block, 1), F32))
        e = jnp.exp2(dot(rows_here, own_opt, NT) * logit_scale)
        rows = s * block + lax.broadcasted_iota(jnp.int32, (block, T), 0)
        columns = my_sar * block + me * T + lax.broadcasted_iota(jnp.int32, (block, T), 1)
        diagonal = (rows == columns).astype(F32)
        coefs = (NCE_SCALE * (e / sums_here - diagonal)).astype(BF16)
        return grad + dot(coefs, rows_here, TN)

    opt_pool_grad = lax.fori_loop(0, n_sar, opt_coefs, jnp.zeros((T, D), F32))

    for which, grad in enumerate((sar_pool_grad, opt_pool_grad)):
        mean = means[which]
        pool_scale = lax.rsqrt(jnp.sum(mean * mean, axis=-1, keepdims=True) + EPSILON)
        pool = pool_rows[which]
        along = jnp.sum(pool * grad, axis=-1, keepdims=True)
        backs[which] = (grad - pool * along) * pool_scale * (1.0 / L)

    def own_at(i, size=ROWS, first=0):
        return pl.ds(pl.multiple_of(i * ROWS + first, 16), size)

    def sar_tile(i, carry):
        own = weights(i)
        put_rows(own_at(i), dot(own, sar_rows[i], NN))
        cands = [opt_rows[i]]
        coefs = [own]
        for k in range(NEG):
            cands.append(fetched[table[SLOT_AT + i * NEG + k]])
            cands.append(fetched_end[table[SLOT_AT + i * NEG + k]])
            coefs.append(weights(T + i * NEG + k))
        pair = dot(jnp.concatenate(coefs, axis=0), jnp.concatenate(cands, axis=0), TN)
        back = backs[0, pl.ds(i, 1), :]
        opt_rows[i] = finish_rows(sar_raw[i].astype(F32), back, pair[0:ROWS]).astype(BF16)
        return carry

    lax.fori_loop(0, T, sar_tile, 0)

    def put_grad(i, values):
        size = values.shape[0]
        for q in range(D // 128):
            by_row[q, pl.ds(i, size, stride=T)] = values[:, q * 128 : (q + 1) * 128]

    writes = []

    def write_grad(which, out, c):
        size = T * (CHUNK if c < CHUNKS else L - MAIN)
        if len(writes) > 1:
            writes[-2].wait()
        slot = len(writes) % 2
        for q in range(D // 128):
            staged[slot, 0:size, q * 128 : (q + 1) * 128] = by_row[q, 0:size].astype(BF16)
        write = pltpu.make_async_copy(
            staged.at[slot, pl.ds(0, size)],
            out.at[pl.ds(c * CHUNK * T, size)],
            write_sem.at[which, c],
        )
        write.start()
        writes.append(write)

    for c in range(CHUNKS + 1):
        at = slice(c * CHUNK, min((c + 1) * CHUNK, ROWS))

        def place_tile(i, carry, at=at):
            put_grad(i, opt_rows[i, at].astype(F32))
            return carry

        lax.fori_loop(0, T, place_tile, 0, unroll=2)
        write_grad(0, sar_out, c)

    sums[SLOTS] = jnp.zeros((CHUNK, D), F32)
    tail_sums[SLOTS] = jnp.zeros((8, D), F32)
    for turn in ORDER:
        back_copy(turn, 1, None).wait_recv()

    def add_tail(t, total):
        place = order2[t]
        both = unpack_ends(returned_tail[place // CAP])
        second = (place % CAP).astype(F32)
        total = total * same2[t].astype(F32) + both[0:8] * (1.0 - second) + both[8:16] * second
        tail_sums[t] = total
        return total

    lax.fori_loop(0, SLOTS, add_tail, jnp.zeros((8, D), F32))

    def opt_tail(j, carry):
        part = tail_sums[last2[j]]
        pair = get_rows(own_at(j, ROWS - MAIN, MAIN)) + jnp.concatenate([part, jnp.zeros_like(part)], axis=0)
        back = backs[1, pl.ds(j, 1), :]
        put_grad(j, finish_rows(opt_raw[j, MAIN:ROWS].astype(F32), back, pair))
        return carry

    lax.fori_loop(0, T, opt_tail, 0)
    write_grad(1, opt_out, CHUNKS)

    for c in range(CHUNKS):
        at = slice(c * CHUNK, (c + 1) * CHUNK)
        for turn in ORDER:
            back_copy(turn, 0, c).wait_recv()
            back_copy(turn, 1, c).wait_recv()

        def add_slot(t, total, c=c):
            total = total * same2[t].astype(F32) + returned[c][order2[t]].astype(F32)
            sums[t] = total
            return total

        lax.fori_loop(0, SLOTS, add_slot, jnp.zeros((CHUNK, D), F32), unroll=2)

        def opt_tile(j, carry, c=c, at=at):
            pair = get_rows(own_at(j, CHUNK, c * CHUNK)) + sums[last2[j]]
            back = backs[1, pl.ds(j, 1), :]
            put_grad(j, finish_rows(opt_raw[j, at].astype(F32), back, pair))
            return carry

        lax.fori_loop(0, T, opt_tile, 0, unroll=2)
        write_grad(1, opt_out, c)

    for turn in ORDER:
        plane_copy(turn).wait_send()
        for c in range(CHUNKS):
            back_copy(turn, 0, c).wait_send()
            back_copy(turn, 1, c).wait_send()
        back_copy(turn, 1, None).wait_send()
    for step in range(1, n_y):
        block_copy(step).wait_send()
    for y in range(n_y):
        mate_copy(y).wait_send()
    for write in writes[-2:]:
        write.wait()


def index_tables(candidates):
    me = lax.axis_index("opt")
    block = T * GROUPS
    local_ids = (candidates % block).reshape(-1)
    hits = (local_ids[:, None] == jnp.arange(block)[None, :]).astype(jnp.int32)
    needed = jnp.max(hits, axis=0).reshape(GROUPS, T)
    rank = jnp.cumsum(needed, axis=1) - needed
    chosen = needed[:, :, None] * (rank[:, :, None] == jnp.arange(128)[None, None, :])
    asked = jnp.sum(chosen * jnp.arange(T)[None, :, None], axis=1)
    pair_rank = jnp.sum(hits * rank.reshape(-1)[None, :], axis=1)
    owner = local_ids // T
    turn = ((me // SIDE - owner // SIDE) % SIDE) * SIDE + (me % SIDE - owner % SIDE) % SIDE
    slot = (turn - 1) * CAP + pair_rank
    turns = jnp.arange(GROUPS)
    owners = ((me // SIDE + turns // SIDE) % SIDE) * SIDE + (me % SIDE + turns % SIDE) % SIDE
    by_turn = jnp.sum(
        (owners[:, None] == jnp.arange(GROUPS)[None, :])[:, :, None] * asked[None], axis=1
    )
    ids = by_turn.astype(jnp.int32)[:, None, :]
    pairs = jnp.arange(PAIRS)
    key = slot * 64 + pairs
    place = jnp.sum(key[None, :] < key[:, None], axis=1)
    at_place = place[None, :] == pairs[:, None]
    sorted_key = jnp.sum(at_place * key[None, :], axis=1)
    sorted_pair, sorted_slot = sorted_key % 64, sorted_key // 64
    same = (sorted_slot == jnp.concatenate([jnp.full((1,), -1), sorted_slot[:-1]])).astype(jnp.int32)
    slots = jnp.arange(SLOTS)
    upto = jnp.sum(slot[None, :] <= slots[:, None], axis=1)
    used = jnp.any(slot[None, :] == slots[:, None], axis=1)
    last = jnp.where(used, upto - 1, PAIRS)
    table = jnp.concatenate(
        [slot, sorted_pair, sorted_pair // NEG, same, last, jnp.zeros((TABLE - LAST_AT - SLOTS,), jnp.int32)]
    )
    return table.astype(jnp.int32), ids


def by_token(tokens):
    return jnp.swapaxes(tokens, 0, 1).reshape(-1, D)


def per_device(n_sar, sar_tokens, opt_tokens, candidates):
    table, ids = index_tables(candidates)
    vmem = pl.BlockSpec(memory_space=pltpu.VMEM)
    hbm = pl.BlockSpec(memory_space=pl.ANY)
    dma = pltpu.SemaphoreType.DMA
    rows = jax.ShapeDtypeStruct((T * L, D), BF16)
    grads = pl.pallas_call(
        functools.partial(kernel, n_sar),
        out_shape=(rows, rows),
        in_specs=[pl.BlockSpec(memory_space=pltpu.SMEM), vmem, hbm, hbm],
        out_specs=[hbm] * 2,
        scratch_shapes=[
            pltpu.VMEM((T, ROWS, D), BF16),
            pltpu.VMEM((T, ROWS, D), BF16),
            pltpu.VMEM((T, LANES, D), BF16),
            pltpu.VMEM((T, ROWS, D), BF16),
            pltpu.VMEM((SLOTS, MAIN, D), BF16),
            pltpu.VMEM((GROUPS - 1, 16, HALF), BF16),
            pltpu.VMEM((SLOTS, FIRST, D), BF16),
            pltpu.VMEM((SLOTS, ROWS - FIRST, D), BF16),
            pltpu.VMEM((GROUPS - 1, 16, HALF), BF16),
            pltpu.VMEM((T + PAIRS, ROWS, LANES), BF16),
            pltpu.VMEM((PAIRS + 1, ROWS, HALF), BF16),
            pltpu.VMEM((ROWS, HALF), F32),
            [pltpu.VMEM((SLOTS, CHUNK, D), BF16)] * CHUNKS,
            pltpu.VMEM((GROUPS - 1, 16, HALF), BF16),
            pltpu.VMEM((GROUPS - 1, 16, HALF), F32),
            pltpu.VMEM((SLOTS + 1, 8, D), F32),
            pltpu.VMEM((n_sar // 2, 2, 2, T * GROUPS, D), BF16),
            pltpu.VMEM((SLOTS + 1, CHUNK, D), F32),
            pltpu.VMEM((D // 128, T * ROWS, 128), F32),
            pltpu.VMEM((2, T, D), F32),
            pltpu.VMEM((2, T, D), F32),
            pltpu.VMEM((2, T, D), F32),
            pltpu.VMEM((NEG + 1, T, LANES), F32),
            pltpu.VMEM((T + PAIRS, 1, LANES), F32),
            pltpu.VMEM((D // 128, T * CHUNK, 128), F32),
            pltpu.VMEM((2, T * CHUNK, D), BF16),
            pltpu.VMEM((GROUPS, 1, 128), jnp.int32),
            pltpu.SMEM((GROUPS, 1, 128), jnp.int32),
            pltpu.SMEM((32,), jnp.int32),
            pltpu.SMEM((32,), jnp.int32),
            pltpu.SMEM((32,), jnp.int32),
            pltpu.SMEM((32,), jnp.int32),
            pltpu.SMEM((32,), jnp.int32),
            dma((GROUPS,)),
            dma((GROUPS,)),
            dma,
            dma((GROUPS, CHUNKS + 1)),
            dma((GROUPS, CHUNKS + 1)),
            dma((GROUPS, 2 * CHUNKS + 1)),
            dma((GROUPS, 2 * CHUNKS + 1)),
            dma((GROUPS,)),
            dma((GROUPS,)),
            dma((n_sar,)),
            dma((n_sar,)),
            dma((2, CHUNKS + 1)),
            dma((2, T)),
        ],
        compiler_params=pltpu.CompilerParams(
            collective_id=0, has_side_effects=True, vmem_limit_bytes=63 * 2**20
        ),
        name="match_grads",
    )(table, ids, by_token(sar_tokens), by_token(opt_tokens))
    return tuple(jnp.swapaxes(grad.reshape(L, T, D), 0, 1) for grad in grads)


def solution(mesh):
    tiles = P(("sar", "opt"), None, None)
    return jax.shard_map(
        functools.partial(per_device, mesh.shape["sar"]),
        mesh=mesh,
        in_specs=(tiles, tiles, P(("sar", "opt"), None)),
        out_specs=(tiles, tiles),
        check_vma=False,
    )
```

```python
import functools

import jax
import jax.numpy as jnp
from jax import lax
from jax.experimental import pallas as pl
from jax.experimental.pallas import tpu as pltpu
from jax.sharding import PartitionSpec as P

NEG = 3
CAP = 2
EPSILON = 1e-06
POOL_TEMP = 0.02
CAND_TEMP = 0.1
NCE_TEMP = 0.07
LOSS_SCALE = 256.0
NCE_SCALE = 0.05 * 256.0 / 0.07
LOG2E = 1.4426950408889634

T = 16
L = 196
D = 512
MAIN = 192
ROWS = 208
LANES = 256
PAIRS = T * NEG
GROUPS = 16
SIDE = 4
SLOTS = (GROUPS - 1) * CAP
CHUNK = 48
CHUNKS = MAIN // CHUNK
HALF = D // 2
FIRST = 3 * CHUNK
ORDER = [10, 2, 8, 6, 14, 9, 11, 5, 7, 13, 15, 1, 3, 4, 12]

SLOT_AT, PAIR_AT, TILE_AT, SAME_AT, LAST_AT, TABLE = 0, 48, 96, 144, 192, 256

BF16 = jnp.bfloat16
F32 = jnp.float32


def negated(turn):
    return ((SIDE - turn // SIDE) % SIDE) * SIDE + (SIDE - turn % SIDE) % SIDE


def dot(a, b, dims):
    return lax.dot_general(a, b, (dims, ((), ())), preferred_element_type=F32)


NN, NT, TN = ((1,), (0,)), ((1,), (1,)), ((0,), (0,))


def inverse_norm(rows):
    return lax.rsqrt(jnp.sum(rows * rows, axis=-1, keepdims=True) + EPSILON)


def finish_rows(raw, back, pair):
    total = pair + back
    inverse = inverse_norm(raw)
    along = jnp.sum(raw * total, axis=-1, keepdims=True)
    return (total - raw * (inverse * inverse * along)) * inverse


def kernel(
    n_sar, table, ids, sar_in, opt_in, sar_out, opt_out,
    sar_raw, opt_raw, sar_rows, opt_rows, outbox, out_tail, fetched, fetched_end, fetched_tail, weight, parts, acc,
    returned, returned_tail, low_ends, tail_sums, pools, sums, own_pair, means, pool_rows, backs, totals,
    scale, by_row, staged, ids_in, ids_smem, keys, ranks, order2, same2, last2,
    ids_send, ids_recv, ids_sem, fetch_send, fetch_recv, back_send, back_recv,
    plane_send, plane_recv, block_send, block_recv, write_sem, read_sem,
):
    my_sar = lax.axis_index("sar")
    me = lax.axis_index("opt")
    my_z, my_x = me // SIDE, me % SIDE

    def peer(turn):
        z = (my_z + turn // SIDE) % SIDE
        x = (my_x + turn % SIDE) % SIDE
        return {"opt": z * SIDE + x}

    n_y = n_sar // 2
    my_y, my_core = my_sar // 2, my_sar % 2

    def y_peer(step):
        return {"sar": ((my_y + step) % n_y) * 2 + my_core}

    mate = {"sar": my_y * 2 + 1 - my_core}

    def remote(src, dst, send, recv, to):
        return pltpu.make_async_remote_copy(
            src_ref=src, dst_ref=dst, send_sem=send, recv_sem=recv,
            device_id=to, device_id_type=pl.DeviceIdType.MESH,
        )

    barrier = pltpu.get_barrier_semaphore()
    for turn in range(1, GROUPS):
        pl.semaphore_signal(
            barrier, inc=1, device_id=peer(turn), device_id_type=pl.DeviceIdType.MESH
        )
    for step in range(1, n_y):
        pl.semaphore_signal(
            barrier, inc=1, device_id=y_peer(step), device_id_type=pl.DeviceIdType.MESH
        )
    pl.semaphore_signal(barrier, inc=1, device_id=mate, device_id_type=pl.DeviceIdType.MESH)

    def reads(which, source, rows):
        span = rows.shape[1]
        copies = []
        for k in range(-(-T * L // span)):
            size = min(span, T * L - k * span)
            copies.append(
                pltpu.make_async_copy(
                    source.at[pl.ds(k * span, size)],
                    rows.at[k, pl.ds(0, size)],
                    read_sem.at[which, k],
                )
            )
        return copies

    opt_reads, sar_reads = reads(1, opt_in, opt_rows), reads(0, sar_in, sar_rows)
    for copy in opt_reads + sar_reads:
        copy.start()

    def put_rows(at, values):
        for q in range(D // 128):
            own_pair[q, at] = values[:, q * 128 : (q + 1) * 128]

    def get_rows(at):
        return jnp.concatenate([own_pair[q, at] for q in range(D // 128)], axis=1)

    put_rows(pl.ds(T * L, T * (ROWS - L)), jnp.zeros((T * (ROWS - L), D), F32))

    def widen_all(copies, rows):
        span = rows.shape[1]
        for copy in copies:
            copy.wait()

        def widen(k, carry):
            put_rows(pl.ds(pl.multiple_of(k * span, 16), span), rows[k].astype(F32))
            return carry

        full = T * L // span
        rest = T * L - full * span
        lax.fori_loop(0, full, widen, 0)
        put_rows(pl.ds(full * span, rest), rows[full, 0:rest].astype(F32))

    def normalize(which, raw, rows, first, size):
        def tile(i, carry):
            values = get_rows(pl.ds(first * T + i, size, stride=T))
            unit = values * inverse_norm(values)
            raw[i, first : first + size] = values.astype(BF16)
            rows[i, first : first + size] = unit.astype(BF16)
            mean = jnp.sum(unit, axis=0, keepdims=True) * (1.0 / L)
            if first == 0:
                means[which, pl.ds(i, 1), :] = mean
            else:
                means[which, pl.ds(i, 1), :] += mean
            return carry

        lax.fori_loop(0, T, tile, 0, unroll=2)

    widen_all(opt_reads, opt_rows)

    pl.semaphore_wait(barrier, GROUPS - 1 + n_y)

    def ids_copy(turn):
        return remote(
            ids.at[turn], ids_in.at[turn], ids_send.at[turn], ids_recv.at[turn], peer(turn)
        )

    for turn in ORDER:
        ids_copy(turn).start()
    normalize(1, opt_raw, opt_rows, 0, CHUNK)
    for turn in ORDER:
        ids_copy(turn).wait()
    to_smem = pltpu.make_async_copy(ids_in, ids_smem, ids_sem)
    to_smem.start()
    to_smem.wait()

    def fetch_copy(turn, c):
        box = pl.ds((turn - 1) * CAP, CAP)
        if c == CHUNKS:
            src, dst = out_tail.at[turn - 1], fetched_tail.at[turn - 1]
        else:
            at = pl.ds(c * CHUNK, CHUNK)
            src = outbox.at[box, at]
            if c * CHUNK < FIRST:
                dst = fetched.at[box, at]
            else:
                dst = fetched_end.at[box, pl.ds(c * CHUNK - FIRST, CHUNK)]
        return remote(src, dst, fetch_send.at[turn, c], fetch_recv.at[turn, c], peer(turn))

    def pack_ends(low, high):
        upper = lax.broadcasted_iota(jnp.int32, (16, HALF), 0) % 8 < 4
        return jnp.where(upper, low, pltpu.roll(high, 4, 0)).astype(BF16)

    def unpack_ends(packed):
        upper = lax.broadcasted_iota(jnp.int32, (16, HALF), 0) % 8 < 4
        packed = packed.astype(F32)
        low = jnp.where(upper, packed, 0.0)
        high = jnp.where(upper, pltpu.roll(packed, 12, 0), 0.0)
        return jnp.concatenate([low, high], axis=1)

    def send_chunk(c):
        for turn in ORDER:
            asker = negated(turn)
            if c < CHUNKS:
                for s in range(CAP):
                    outbox[(turn - 1) * CAP + s, c * CHUNK : (c + 1) * CHUNK] = opt_rows[
                        ids_smem[asker, 0, s], c * CHUNK : (c + 1) * CHUNK
                    ]
            else:
                ends = [
                    opt_rows[ids_smem[asker, 0, s], MAIN:ROWS].astype(F32)[0:8] for s in range(CAP)
                ]
                both = jnp.concatenate(ends, axis=0)
                out_tail[turn - 1] = pack_ends(both[:, :HALF], both[:, HALF:])
            fetch_copy(turn, c).start()

    send_chunk(0)

    normalize(1, opt_raw, opt_rows, CHUNK, ROWS - CHUNK)
    widen_all(sar_reads, sar_rows)
    normalize(0, sar_raw, sar_rows, 0, ROWS)

    def clear(i, carry):
        sar_rows[i, ROWS:LANES] = jnp.zeros((LANES - ROWS, D), BF16)
        return carry

    lax.fori_loop(0, T, clear, 0)

    mine = pl.ds(pl.multiple_of(me * T, T), T)
    for which in range(2):
        mean = means[which]
        pool_scale = lax.rsqrt(jnp.sum(mean * mean, axis=-1, keepdims=True) + EPSILON)
        pool = mean * pool_scale
        pool_rows[which] = pool
        pools[my_y, my_core, which, mine, :] = pool.astype(BF16)

    def plane_copy(turn):
        here = pools.at[my_y, my_core, :, mine, :]
        return remote(here, here, plane_send.at[turn], plane_recv.at[turn], peer(turn))

    for turn in ORDER:
        plane_copy(turn).start()

    send_chunk(1)

    def exp_scores(rows, i):
        return jnp.exp2(dot(rows, sar_rows[i], NT) * (LOG2E / POOL_TEMP))

    live = lax.broadcasted_iota(jnp.int32, (ROWS, LANES), 0) < L

    def own_scores(i, carry):
        e = exp_scores(opt_rows[i], i)
        weight[i] = e.astype(BF16)
        totals[0, pl.ds(i, 1), :] = jnp.sum(jnp.where(live, e, 0.0), axis=0, keepdims=True)
        return carry

    lax.fori_loop(0, T, own_scores, 0)

    for p in range(SLOTS):
        keys[p] = ids_smem[p // CAP + 1, 0, p % CAP] * 32 + p

    def rank_of(p, carry):
        key = keys[p]
        rank = jnp.int32(0)
        for q in range(SLOTS):
            rank += (keys[q] < key).astype(jnp.int32)
        ranks[p] = rank
        return carry

    lax.fori_loop(0, SLOTS, rank_of, 0)

    def place_of(t, before):
        key = jnp.int32(0)
        for p in range(SLOTS):
            key += jnp.where(ranks[p] == t, keys[p], 0)
        tile = key // 32
        order2[t] = key % 32
        same2[t] = (tile == before).astype(jnp.int32)
        return tile

    lax.fori_loop(0, SLOTS, place_of, jnp.int32(-1))

    def last_of(j, before):
        upto = jnp.int32(0)
        for p in range(SLOTS):
            upto += (keys[p] < (j + 1) * 32).astype(jnp.int32)
        last2[j] = jnp.where(upto > before, upto - 1, SLOTS)
        return upto

    lax.fori_loop(0, T, last_of, jnp.int32(0))

    for turn in ORDER:
        plane_copy(turn).wait_recv()

    def block_copy(step):
        here = pools.at[my_y, my_core]
        return remote(here, here, block_send.at[step], block_recv.at[step], y_peer(step))

    def mate_copy(y):
        here = pools.at[y, my_core]
        return remote(here, here, block_send.at[n_y + y], block_recv.at[n_y + y], mate)

    for step in range(1, n_y):
        block_copy(step).start()
        if step + 1 < CHUNKS:
            send_chunk(step + 1)
    for c in range(n_y, CHUNKS + 1):
        send_chunk(c)

    for c in range(FIRST // CHUNK):
        for turn in ORDER:
            fetch_copy(turn, c).wait_recv()

    def first_scores(i, carry):
        rows = [fetched[table[SLOT_AT + i * NEG + k]] for k in range(NEG)]
        exps = exp_scores(jnp.concatenate(rows, axis=0), i)
        for k in range(NEG):
            e = exps[k * FIRST : (k + 1) * FIRST]
            weight[T + i * NEG + k, 0:FIRST] = e.astype(BF16)
            totals[k + 1, pl.ds(i, 1), :] = jnp.sum(e, axis=0, keepdims=True)
        return carry

    lax.fori_loop(0, T, first_scores, 0)

    for c in range(FIRST // CHUNK, CHUNKS + 1):
        for turn in ORDER:
            fetch_copy(turn, c).wait_recv()
    for turn in range(1, GROUPS):
        ends = unpack_ends(fetched_tail[turn - 1])
        for s in range(CAP):
            end = ends[8 * s : 8 * s + 8]
            fetched_end[(turn - 1) * CAP + s, MAIN - FIRST :] = jnp.concatenate(
                [end, jnp.zeros_like(end)], axis=0
            ).astype(BF16)

    live_end = lax.broadcasted_iota(jnp.int32, (ROWS - FIRST, LANES), 0) < L - FIRST

    def last_scores(i, carry):
        rows = [fetched_end[table[SLOT_AT + i * NEG + k]] for k in range(NEG)]
        exps = exp_scores(jnp.concatenate(rows, axis=0), i)
        for k in range(NEG):
            e = exps[k * (ROWS - FIRST) : (k + 1) * (ROWS - FIRST)]
            weight[T + i * NEG + k, FIRST:ROWS] = e.astype(BF16)
            totals[k + 1, pl.ds(i, 1), :] += jnp.sum(
                jnp.where(live_end, e, 0.0), axis=0, keepdims=True
            )
        return carry

    lax.fori_loop(0, T, last_scores, 0, unroll=4)

    for step in range(1, n_y):
        block_copy(step).wait_recv()
    for y in range(n_y):
        mate_copy(y).start()

    tokens = lax.broadcasted_iota(jnp.int32, (T, LANES), 1) < L
    cand = []
    for k in range(NEG + 1):
        logs = jnp.where(tokens, jnp.log(totals[k]), 0.0)
        match = (POOL_TEMP / L) * jnp.sum(logs, axis=-1, keepdims=True)
        cand.append(jnp.exp(match / CAND_TEMP))
    cand_sum = cand[0] + cand[1] + cand[2] + cand[3]
    for k in range(NEG + 1):
        coef = LOSS_SCALE * (cand[k] / cand_sum - (1.0 if k == 0 else 0.0)) / CAND_TEMP
        scaled = (coef / L) / totals[k]
        for i in range(T):
            scale[i if k == 0 else T + i * NEG + k - 1] = scaled[i : i + 1]

    def weights(p):
        return (weight[p].astype(F32) * scale[p]).astype(BF16)

    def back_copy(turn, h, c):
        box = pl.ds((turn - 1) * CAP, CAP)
        if c is None:
            src, dst = out_tail.at[turn - 1], returned_tail.at[turn - 1]
            sem = 2 * CHUNKS
        else:
            at, cols = pl.ds(c * CHUNK, CHUNK), pl.ds(h * HALF, HALF)
            src, dst = outbox.at[box, at, cols], returned[c].at[box, :, cols]
            sem = h * CHUNKS + c
        return remote(src, dst, back_send.at[turn, sem], back_recv.at[turn, sem], peer(turn))

    parts[PAIRS] = jnp.zeros((ROWS, HALF), BF16)
    for c in range(CHUNKS + 1):
        for turn in ORDER:
            fetch_copy(turn, c).wait_send()
    for h in range(2):
        cols = slice(h * HALF, (h + 1) * HALF)
        acc[...] = jnp.zeros_like(acc)

        def add_pair(p, carry, cols=cols):
            pair = table[PAIR_AT + p]
            keep = table[SAME_AT + p].astype(F32)
            part = dot(weights(T + pair), sar_rows[table[TILE_AT + p], :, cols], NN)
            total = acc[...] * keep + part
            acc[...] = total
            parts[p] = total.astype(BF16)
            return carry

        lax.fori_loop(0, PAIRS, add_pair, 0, unroll=4)

        def send_tails(h=h, cols=cols):
            for turn in ORDER:
                ends = [
                    parts[table[LAST_AT + (negated(turn) - 1) * CAP + s], MAIN:ROWS].astype(F32)[0:8]
                    for s in range(CAP)
                ]
                both = jnp.concatenate(ends, axis=0)
                if h:
                    out_tail[turn - 1] = pack_ends(low_ends[turn - 1], both)
                    back_copy(turn, h, None).start()
                else:
                    low_ends[turn - 1] = both

        if h:
            send_tails()
        for c in range(CHUNKS):
            at = slice(c * CHUNK, (c + 1) * CHUNK)
            for turn in ORDER:
                for s in range(CAP):
                    last = table[LAST_AT + (negated(turn) - 1) * CAP + s]
                    outbox[(turn - 1) * CAP + s, at, cols] = parts[last, at, :]
                back_copy(turn, h, c).start()
        if not h:
            send_tails()

    for y in range(n_y):
        mate_copy(y).wait_recv()
    block = pools.shape[3]
    logit_scale = LOG2E / NCE_TEMP
    own_sar = pools[my_y, my_core, 0, mine, :]
    own_opt = pools[my_y, my_core, 1, mine, :]

    def own_rows(t, row_sums):
        e = jnp.exp2(dot(own_sar, pools[t // 2, t % 2, 1], NT) * logit_scale)
        return row_sums + jnp.sum(e, axis=-1, keepdims=True)

    row_sums = lax.fori_loop(0, n_sar, own_rows, jnp.zeros((T, 1), F32))

    def own_coefs(t, grad):
        e = jnp.exp2(dot(own_sar, pools[t // 2, t % 2, 1], NT) * logit_scale)
        rows = my_sar * block + me * T + lax.broadcasted_iota(jnp.int32, (T, block), 0)
        columns = t * block + lax.broadcasted_iota(jnp.int32, (T, block), 1)
        diagonal = (rows == columns).astype(F32)
        coefs = (NCE_SCALE * (e / row_sums - diagonal)).astype(BF16)
        return grad + dot(coefs, pools[t // 2, t % 2, 1], NN)

    sar_pool_grad = lax.fori_loop(0, n_sar, own_coefs, jnp.zeros((T, D), F32))

    def opt_coefs(s, grad):
        rows_here = pools[s // 2, s % 2, 0]

        def add_sums(t, sums_here):
            e = jnp.exp2(dot(rows_here, pools[t // 2, t % 2, 1], NT) * logit_scale)
            return sums_here + jnp.sum(e, axis=-1, keepdims=True)

        sums_here = lax.fori_loop(0, n_sar, add_sums, jnp.zeros((block, 1), F32))
        e = jnp.exp2(dot(rows_here, own_opt, NT) * logit_scale)
        rows = s * block + lax.broadcasted_iota(jnp.int32, (block, T), 0)
        columns = my_sar * block + me * T + lax.broadcasted_iota(jnp.int32, (block, T), 1)
        diagonal = (rows == columns).astype(F32)
        coefs = (NCE_SCALE * (e / sums_here - diagonal)).astype(BF16)
        return grad + dot(coefs, rows_here, TN)

    opt_pool_grad = lax.fori_loop(0, n_sar, opt_coefs, jnp.zeros((T, D), F32))

    for which, grad in enumerate((sar_pool_grad, opt_pool_grad)):
        mean = means[which]
        pool_scale = lax.rsqrt(jnp.sum(mean * mean, axis=-1, keepdims=True) + EPSILON)
        pool = pool_rows[which]
        along = jnp.sum(pool * grad, axis=-1, keepdims=True)
        backs[which] = (grad - pool * along) * pool_scale * (1.0 / L)

    def own_at(i, size=ROWS, first=0):
        return pl.ds(pl.multiple_of(i * ROWS + first, 16), size)

    def sar_tile(i, carry):
        own = weights(i)
        put_rows(own_at(i), dot(own, sar_rows[i], NN))
        cands = [opt_rows[i]]
        coefs = [own]
        for k in range(NEG):
            cands.append(fetched[table[SLOT_AT + i * NEG + k]])
            cands.append(fetched_end[table[SLOT_AT + i * NEG + k]])
            coefs.append(weights(T + i * NEG + k))
        pair = dot(jnp.concatenate(coefs, axis=0), jnp.concatenate(cands, axis=0), TN)
        back = backs[0, pl.ds(i, 1), :]
        opt_rows[i] = finish_rows(sar_raw[i].astype(F32), back, pair[0:ROWS]).astype(BF16)
        return carry

    lax.fori_loop(0, T, sar_tile, 0)

    def put_grad(i, values):
        size = values.shape[0]
        for q in range(D // 128):
            by_row[q, pl.ds(i, size, stride=T)] = values[:, q * 128 : (q + 1) * 128]

    writes = []

    def write_grad(which, out, c):
        size = T * (CHUNK if c < CHUNKS else L - MAIN)
        if len(writes) > 1:
            writes[-2].wait()
        slot = len(writes) % 2
        for q in range(D // 128):
            staged[slot, 0:size, q * 128 : (q + 1) * 128] = by_row[q, 0:size].astype(BF16)
        write = pltpu.make_async_copy(
            staged.at[slot, pl.ds(0, size)],
            out.at[pl.ds(c * CHUNK * T, size)],
            write_sem.at[which, c],
        )
        write.start()
        writes.append(write)

    for c in range(CHUNKS + 1):
        at = slice(c * CHUNK, min((c + 1) * CHUNK, ROWS))

        def place_tile(i, carry, at=at):
            put_grad(i, opt_rows[i, at].astype(F32))
            return carry

        lax.fori_loop(0, T, place_tile, 0, unroll=2)
        write_grad(0, sar_out, c)

    sums[SLOTS] = jnp.zeros((CHUNK, D), F32)
    tail_sums[SLOTS] = jnp.zeros((8, D), F32)
    for turn in ORDER:
        back_copy(turn, 1, None).wait_recv()

    def add_tail(t, total):
        place = order2[t]
        both = unpack_ends(returned_tail[place // CAP])
        second = (place % CAP).astype(F32)
        total = total * same2[t].astype(F32) + both[0:8] * (1.0 - second) + both[8:16] * second
        tail_sums[t] = total
        return total

    lax.fori_loop(0, SLOTS, add_tail, jnp.zeros((8, D), F32))

    def opt_tail(j, carry):
        part = tail_sums[last2[j]]
        pair = get_rows(own_at(j, ROWS - MAIN, MAIN)) + jnp.concatenate([part, jnp.zeros_like(part)], axis=0)
        back = backs[1, pl.ds(j, 1), :]
        put_grad(j, finish_rows(opt_raw[j, MAIN:ROWS].astype(F32), back, pair))
        return carry

    lax.fori_loop(0, T, opt_tail, 0)
    write_grad(1, opt_out, CHUNKS)

    for c in range(CHUNKS):
        at = slice(c * CHUNK, (c + 1) * CHUNK)
        for turn in ORDER:
            back_copy(turn, 0, c).wait_recv()
            back_copy(turn, 1, c).wait_recv()

        def add_slot(t, total, c=c):
            total = total * same2[t].astype(F32) + returned[c][order2[t]].astype(F32)
            sums[t] = total
            return total

        lax.fori_loop(0, SLOTS, add_slot, jnp.zeros((CHUNK, D), F32), unroll=2)

        def opt_tile(j, carry, c=c, at=at):
            pair = get_rows(own_at(j, CHUNK, c * CHUNK)) + sums[last2[j]]
            back = backs[1, pl.ds(j, 1), :]
            put_grad(j, finish_rows(opt_raw[j, at].astype(F32), back, pair))
            return carry

        lax.fori_loop(0, T, opt_tile, 0, unroll=4)
        write_grad(1, opt_out, c)

    for turn in ORDER:
        plane_copy(turn).wait_send()
        for c in range(CHUNKS):
            back_copy(turn, 0, c).wait_send()
            back_copy(turn, 1, c).wait_send()
        back_copy(turn, 1, None).wait_send()
    for step in range(1, n_y):
        block_copy(step).wait_send()
    for y in range(n_y):
        mate_copy(y).wait_send()
    for write in writes[-2:]:
        write.wait()


def index_tables(candidates):
    me = lax.axis_index("opt")
    block = T * GROUPS
    local_ids = (candidates % block).reshape(-1)
    hits = (local_ids[:, None] == jnp.arange(block)[None, :]).astype(jnp.int32)
    needed = jnp.max(hits, axis=0).reshape(GROUPS, T)
    rank = jnp.cumsum(needed, axis=1) - needed
    chosen = needed[:, :, None] * (rank[:, :, None] == jnp.arange(128)[None, None, :])
    asked = jnp.sum(chosen * jnp.arange(T)[None, :, None], axis=1)
    pair_rank = jnp.sum(hits * rank.reshape(-1)[None, :], axis=1)
    owner = local_ids // T
    turn = ((me // SIDE - owner // SIDE) % SIDE) * SIDE + (me % SIDE - owner % SIDE) % SIDE
    slot = (turn - 1) * CAP + pair_rank
    turns = jnp.arange(GROUPS)
    owners = ((me // SIDE + turns // SIDE) % SIDE) * SIDE + (me % SIDE + turns % SIDE) % SIDE
    by_turn = jnp.sum(
        (owners[:, None] == jnp.arange(GROUPS)[None, :])[:, :, None] * asked[None], axis=1
    )
    ids = by_turn.astype(jnp.int32)[:, None, :]
    pairs = jnp.arange(PAIRS)
    key = slot * 64 + pairs
    place = jnp.sum(key[None, :] < key[:, None], axis=1)
    at_place = place[None, :] == pairs[:, None]
    sorted_key = jnp.sum(at_place * key[None, :], axis=1)
    sorted_pair, sorted_slot = sorted_key % 64, sorted_key // 64
    same = (sorted_slot == jnp.concatenate([jnp.full((1,), -1), sorted_slot[:-1]])).astype(jnp.int32)
    slots = jnp.arange(SLOTS)
    upto = jnp.sum(slot[None, :] <= slots[:, None], axis=1)
    used = jnp.any(slot[None, :] == slots[:, None], axis=1)
    last = jnp.where(used, upto - 1, PAIRS)
    table = jnp.concatenate(
        [slot, sorted_pair, sorted_pair // NEG, same, last, jnp.zeros((TABLE - LAST_AT - SLOTS,), jnp.int32)]
    )
    return table.astype(jnp.int32), ids


def by_token(tokens):
    return jnp.swapaxes(tokens, 0, 1).reshape(-1, D)


def per_device(n_sar, sar_tokens, opt_tokens, candidates):
    table, ids = index_tables(candidates)
    vmem = pl.BlockSpec(memory_space=pltpu.VMEM)
    hbm = pl.BlockSpec(memory_space=pl.ANY)
    dma = pltpu.SemaphoreType.DMA
    rows = jax.ShapeDtypeStruct((T * L, D), BF16)
    grads = pl.pallas_call(
        functools.partial(kernel, n_sar),
        out_shape=(rows, rows),
        in_specs=[pl.BlockSpec(memory_space=pltpu.SMEM), vmem, hbm, hbm],
        out_specs=[hbm] * 2,
        scratch_shapes=[
            pltpu.VMEM((T, ROWS, D), BF16),
            pltpu.VMEM((T, ROWS, D), BF16),
            pltpu.VMEM((T, LANES, D), BF16),
            pltpu.VMEM((T, ROWS, D), BF16),
            pltpu.VMEM((SLOTS, MAIN, D), BF16),
            pltpu.VMEM((GROUPS - 1, 16, HALF), BF16),
            pltpu.VMEM((SLOTS, FIRST, D), BF16),
            pltpu.VMEM((SLOTS, ROWS - FIRST, D), BF16),
            pltpu.VMEM((GROUPS - 1, 16, HALF), BF16),
            pltpu.VMEM((T + PAIRS, ROWS, LANES), BF16),
            pltpu.VMEM((PAIRS + 1, ROWS, HALF), BF16),
            pltpu.VMEM((ROWS, HALF), F32),
            [pltpu.VMEM((SLOTS, CHUNK, D), BF16)] * CHUNKS,
            pltpu.VMEM((GROUPS - 1, 16, HALF), BF16),
            pltpu.VMEM((GROUPS - 1, 16, HALF), F32),
            pltpu.VMEM((SLOTS + 1, 8, D), F32),
            pltpu.VMEM((n_sar // 2, 2, 2, T * GROUPS, D), BF16),
            pltpu.VMEM((SLOTS + 1, CHUNK, D), F32),
            pltpu.VMEM((D // 128, T * ROWS, 128), F32),
            pltpu.VMEM((2, T, D), F32),
            pltpu.VMEM((2, T, D), F32),
            pltpu.VMEM((2, T, D), F32),
            pltpu.VMEM((NEG + 1, T, LANES), F32),
            pltpu.VMEM((T + PAIRS, 1, LANES), F32),
            pltpu.VMEM((D // 128, T * CHUNK, 128), F32),
            pltpu.VMEM((2, T * CHUNK, D), BF16),
            pltpu.VMEM((GROUPS, 1, 128), jnp.int32),
            pltpu.SMEM((GROUPS, 1, 128), jnp.int32),
            pltpu.SMEM((32,), jnp.int32),
            pltpu.SMEM((32,), jnp.int32),
            pltpu.SMEM((32,), jnp.int32),
            pltpu.SMEM((32,), jnp.int32),
            pltpu.SMEM((32,), jnp.int32),
            dma((GROUPS,)),
            dma((GROUPS,)),
            dma,
            dma((GROUPS, CHUNKS + 1)),
            dma((GROUPS, CHUNKS + 1)),
            dma((GROUPS, 2 * CHUNKS + 1)),
            dma((GROUPS, 2 * CHUNKS + 1)),
            dma((GROUPS,)),
            dma((GROUPS,)),
            dma((n_sar,)),
            dma((n_sar,)),
            dma((2, CHUNKS + 1)),
            dma((2, T)),
        ],
        compiler_params=pltpu.CompilerParams(
            collective_id=0, has_side_effects=True, vmem_limit_bytes=63 * 2**20
        ),
        name="match_grads",
    )(table, ids, by_token(sar_tokens), by_token(opt_tokens))
    return tuple(jnp.swapaxes(grad.reshape(L, T, D), 0, 1) for grad in grads)


def solution(mesh):
    tiles = P(("sar", "opt"), None, None)
    return jax.shard_map(
        functools.partial(per_device, mesh.shape["sar"]),
        mesh=mesh,
        in_specs=(tiles, tiles, P(("sar", "opt"), None)),
        out_specs=(tiles, tiles),
        check_vma=False,
    )
```
